128 devices in a mesh: slab: 4 (over x), dev: 32 (over z, y, core).
Axes of the slice: x: 4, y: 4, z: 4, core: 2. Of those that a mesh axis runs over, the one named last changes fastest.
Arguments:
- table: float32 [524288, 128], P(('slab', 'dev')), may hold values from -6 to 6
- accum: float32 [524288, 128], P(('slab', 'dev')), may hold values from 0.1 to 1
- evict_delta: float32 [128, 128, 4, 128], P(('slab', 'dev')), may hold values from -6 to 6
- evict_ids: int32 [128, 128, 4], P(('slab', 'dev')), may hold values from 0 to 4095
- hot_ids: int32 [128, 16], P(('slab', 'dev')), may hold values from 0 to 4095
- cache_old: bfloat16 [2048, 128], replicated, may hold values from -6 to 6
- bag_index: int32 [65536, 16, 8], P(('slab', 'dev')), may hold values from 0 to 4095
- bag_length: int32 [65536, 16], P(('slab', 'dev')), may hold values from 1 to 8
- labels: int32 [65536], P(('slab', 'dev')), may hold values 0 or 1
- w_first: bfloat16 [2048, 2048], P(('slab', 'dev')), may hold values from -0.125 to 0.125
- w_out: bfloat16 [2048], replicated, may hold values from -0.125 to 0.125
Outputs:
- table_new: float32 [524288, 128], P(('slab', 'dev'))
- accum_new: float32 [524288, 128], P(('slab', 'dev'))
- grad_w1: float32 [2048, 2048], P(('slab', 'dev'))
- grad_w2: float32 [2048], replicated
The draws below stay inside these ranges and needn't reach their ends.
All inputs are finite; a program needn't handle non-finite values. No bound on the sum of `labels` on one device may be relied on, other than what follows from the above.
Results may differ from the reference program's by a relative error of at most 0.003.
Values may be sent and summed in bfloat16 or wider, within the bound.
No kernel may reach another device: no remote copies, remote signals or barrier semaphores. Data moves between devices by JAX's collectives and lax.ppermute only.
A program may use at most 128 MiB of HBM per device.

```python
import math
import jax
import jax.numpy as jnp
from jax import lax

E = 128
F = 16
H = 2048
L = 8
R_DEV = 4096
CAP = 4
HOT_DEV = 16
C_OLD = 2048
B_DEV = 512
ROWS = 524288
NEW = 2048
TOKENS = 65536
N_SLAB = 4
N_DEV = 32
DEVICES = 128


def set_ends(drawn, key, least, high):
    longest = drawn.shape.index(max(drawn.shape))
    spots = []
    for shift in (0, 1):
        where = [jax.random.randint(jax.random.fold_in(key, axis), (), 0, length) for axis, length in enumerate(drawn.shape)]
        where[longest] = (where[longest] + shift) % drawn.shape[longest]
        spots.append(tuple(where))
    return drawn.at[spots[0]].set(least).at[spots[1]].set(high)


def level_of(key, extent, shards, smallest, top_value):
    gain = 1.0
    for dim, shards_of in shards:
        draws = jax.random.uniform(jax.random.fold_in(jax.random.fold_in(key, 6), dim), (shards_of,), jnp.float32, smallest / len(shards), top_value / len(shards))
        gain = gain * jnp.repeat(jnp.exp(draws), extent[dim] // shards_of).reshape((-1,) + (1,) * (len(extent) - 1 - dim))
    return gain


def centred(key, extent, width, most, pieces=(), kind=jnp.bfloat16):
    array = jax.random.normal(key, extent, jnp.float32) * width
    if len(pieces) > 0:
        array = level_of(key, extent, pieces, -0.22, 0.18) * array
    return jnp.clip(array, min=-most, max=most).astype(kind)


def setup_inputs(seed: int = 0) -> dict:
    key_of = jax.random.split(jax.random.key(seed), 12)
    table = centred(key_of[0], (ROWS, E), 1.0, 6.0, ((0, 128),), jnp.float32)
    accum = jnp.clip(jnp.exp(math.log(1.0) - 2.3025851 * jax.random.uniform(key_of[1], (ROWS, E), jnp.float32) ** level_of(key_of[1], (ROWS, E), ((0, 128),), -0.2, 0.2)), 0.1, 1.0)
    evict_delta = centred(key_of[2], (N_SLAB * N_DEV, N_SLAB * N_DEV, CAP, E), 1.0, 6.0, ((0, 128),), jnp.float32)
    evict_ids = set_ends(jax.random.randint(key_of[3], (N_SLAB * N_DEV, N_SLAB * N_DEV, CAP), 0, R_DEV), jax.random.fold_in(key_of[3], 1), 0, R_DEV - 1).astype(jnp.int32)
    hot_ids = set_ends(jax.random.randint(key_of[4], (N_SLAB * N_DEV, HOT_DEV), 0, R_DEV), jax.random.fold_in(key_of[4], 1), 0, R_DEV - 1).astype(jnp.int32)
    cache_old = centred(key_of[5], (C_OLD, E), 1.0, 6.0)
    bag_index = set_ends(jax.random.randint(key_of[6], (TOKENS, F, L), 0, C_OLD + NEW), jax.random.fold_in(key_of[6], 1), 0, (C_OLD + NEW) - 1).astype(jnp.int32)
    bag_length = set_ends(jax.random.randint(key_of[7], (TOKENS, F), 1, L + 1), jax.random.fold_in(key_of[7], 1), 1, L).astype(jnp.int32)
    labels = set_ends((jax.random.randint(key_of[8], (TOKENS,), 0, 2) < 1).astype(jnp.int32), jax.random.fold_in(key_of[8], 1), 0, 1)
    w_first = centred(key_of[9], (F * E, H), (F * E) ** -0.5, 0.125, ((0, 128),))
    w_out = centred(key_of[10], (H,), H ** -0.5, 0.125)
    return {"table": table, "accum": accum, "evict_delta": evict_delta, "evict_ids": evict_ids, "hot_ids": hot_ids, "cache_old": cache_old, "bag_index": bag_index, "bag_length": bag_length, "labels": labels, "w_first": w_first, "w_out": w_out}


def gelu_tanh(values):
    return jax.nn.gelu(values, approximate=True)

def reference(table, accum, evict_delta, evict_ids, hot_ids, cache_old, bag_index, bag_length, labels, w_first, w_out):
    owners = jnp.arange(DEVICES, dtype=jnp.int32)
    flat_ids = (evict_ids + owners[None, :, None] * R_DEV).reshape(-1).astype(jnp.int32)
    summed = jnp.zeros_like(table).at[flat_ids].add(evict_delta.reshape(-1, E))
    accum_new = accum + summed * summed
    table_new = table - 0.5 * summed * lax.rsqrt(accum_new)
    hot_flat = (hot_ids + owners[:, None] * R_DEV).reshape(-1).astype(jnp.int32)
    new_rows = table_new[hot_flat].astype(jnp.bfloat16)
    cache_all = jnp.concatenate([cache_old, new_rows], axis=0)
    out_w = w_out.astype(jnp.float32)

    def block(carry, inputs):
        indices, lengths, marks = inputs
        pooled_sum = jnp.zeros((B_DEV, F, E), jnp.float32)
        for position in range(L):
            gathered = jnp.take(cache_all, indices[:, :, position], axis=0).astype(jnp.float32)
            live = (position < lengths)[:, :, None]
            pooled_sum = pooled_sum + jnp.where(live, gathered, 0.0)
        pooled = pooled_sum.reshape(B_DEV, F * E).astype(jnp.bfloat16)
        hidden = jnp.dot(pooled, w_first, preferred_element_type=jnp.float32)
        act, backward = jax.vjp(gelu_tanh, hidden)
        slope = backward(jnp.ones_like(hidden))[0]
        act_b = act.astype(jnp.bfloat16)
        logit = jnp.dot(act_b, w_out, preferred_element_type=jnp.float32)
        grad_logit = 0.125 * (jax.nn.sigmoid(logit) - marks.astype(jnp.float32))
        grad_hidden = (grad_logit[:, None] * out_w[None, :] * slope).astype(jnp.bfloat16)
        first = carry[0] + jnp.dot(pooled.T, grad_hidden, preferred_element_type=jnp.float32)
        second = carry[1] + jnp.dot(grad_logit, act_b.astype(jnp.float32))
        return ((first, second), None)
    init = (jnp.zeros((F * E, H), jnp.float32), jnp.zeros((H,), jnp.float32))
    (grad_w1, grad_w2), _ = lax.scan(block, init, (bag_index.reshape(DEVICES, B_DEV, F, L), bag_length.reshape(DEVICES, B_DEV, F), labels.reshape(DEVICES, B_DEV)))
    return (table_new, accum_new, grad_w1, grad_w2)
```

```python
import jax
import jax.numpy as jnp
from jax import lax
from jax.experimental import pallas as pl
from jax.experimental.pallas import tpu as pltpu
from jax.sharding import Mesh
from jax.sharding import PartitionSpec as P

ALL = ("x", "z", "y", "core")
CHIPS = ("x", "z", "y")
SWAP = ((0, 1), (1, 0))
N_ALL = 128
N_CHIPS = 64
LO = 256
FIELDS = 8
SHIFT = 2.0 ** 24


def split_index(idx, length):
    most, samples = idx.shape
    live = lax.broadcasted_iota(jnp.int32, idx.shape, 0) < length
    low = idx & (LO - 1)
    high = idx >> 8
    unit = jnp.int32(1) << (4 * (high & 7))
    old = jnp.where(live & (high < 8), unit, 0)
    new = jnp.where(live & (high >= 8), unit, 0)
    return low, old, new


def field_counts(word, k):
    if k == FIELDS - 1:
        return lax.shift_right_logical(word, 28).astype(jnp.float32)
    return (word & (15 << (4 * k))).astype(jnp.float32)


def count_kernel(idx_ref, len_ref, told_ref, words_ref, part_ref, low_ref, old_ref, new_ref, c_ref):
    most, samples = idx_ref.shape[1:]
    low, old, new = split_index(idx_ref[0], len_ref[0])
    for j in range(most):
        rows = slice(8 * j, 8 * j + 8)
        low_ref[rows] = jnp.broadcast_to(low[j : j + 1], (8, samples))
        old_ref[rows] = jnp.broadcast_to(old[j : j + 1], (8, samples))
        new_ref[rows] = jnp.broadcast_to(new[j : j + 1], (8, samples))
    line = lax.broadcasted_iota(jnp.int32, (8, 128), 0)

    def chunk(step, carry):
        base = pl.multiple_of(step * 32, 32)
        for lane in range(samples // 128):
            lanes = slice(128 * lane, 128 * lane + 128)
            a_old = [jnp.zeros((8, 128), jnp.int32) for _ in range(4)]
            a_new = [jnp.zeros((8, 128), jnp.int32) for _ in range(4)]
            for j in range(most):
                rows = slice(8 * j, 8 * j + 8)
                lo = low_ref[rows, lanes] - base
                v_old = old_ref[rows, lanes]
                v_new = new_ref[rows, lanes]
                for t in range(4):
                    hit = lo == line + 8 * t
                    a_old[t] = a_old[t] + jnp.where(hit, v_old, 0)
                    a_new[t] = a_new[t] + jnp.where(hit, v_new, 0)
            words_ref[0, pl.ds(base, 32), lanes] = jnp.concatenate(a_new, axis=0)
            word = jnp.concatenate(a_old, axis=0)
            for k in range(FIELDS):
                c_ref[pl.ds(pl.multiple_of(LO * k + base, 32), 32), lanes] = field_counts(word, k).astype(jnp.bfloat16)
        return carry

    lax.fori_loop(0, LO // 32, chunk, 0)
    part_ref[0] = jnp.dot(told_ref[...], c_ref[...], preferred_element_type=jnp.float32)


def count_call(idx, length, told):
    fields, most, samples = idx.shape
    width = told.shape[0]
    return pl.pallas_call(
        count_kernel,
        grid=(fields,),
        in_specs=[
            pl.BlockSpec((1, most, samples), lambda f: (f, 0, 0)),
            pl.BlockSpec((1, 1, samples), lambda f: (f, 0, 0)),
            pl.BlockSpec(told.shape, lambda f: (0, 0)),
        ],
        out_specs=[
            pl.BlockSpec((1, LO, samples), lambda f: (f, 0, 0)),
            pl.BlockSpec((1, width, samples), lambda f: (f, 0, 0)),
        ],
        out_shape=[
            jax.ShapeDtypeStruct((fields, LO, samples), jnp.int32),
            jax.ShapeDtypeStruct((fields, width, samples), jnp.float32),
        ],
        scratch_shapes=[
            pltpu.VMEM((8 * most, samples), jnp.int32),
            pltpu.VMEM((8 * most, samples), jnp.int32),
            pltpu.VMEM((8 * most, samples), jnp.int32),
            pltpu.VMEM((LO * FIELDS, samples), jnp.bfloat16),
        ],
        compiler_params=pltpu.CompilerParams(vmem_limit_bytes=32 * 1024 * 1024),
        cost_estimate=pl.CostEstimate(flops=2 * fields * samples * 2048 * 128, bytes_accessed=20 << 20, transcendentals=0),
        name="count_bags",
    )(idx, length.reshape(fields, 1, samples), told)


def new_kernel(words_ref, part_ref, tnew_ref, pooled_ref, c_ref):
    samples = words_ref.shape[2]

    def chunk(step, carry):
        base = pl.multiple_of(step * 32, 32)
        for lane in range(samples // 128):
            lanes = slice(128 * lane, 128 * lane + 128)
            word = words_ref[0, pl.ds(base, 32), lanes]
            for k in range(FIELDS):
                c_ref[pl.ds(pl.multiple_of(LO * k + base, 32), 32), lanes] = field_counts(word, k).astype(jnp.bfloat16)
        return carry

    lax.fori_loop(0, LO // 32, chunk, 0)
    new = jnp.dot(tnew_ref[...], c_ref[...], preferred_element_type=jnp.float32)
    pooled_ref[...] = ((part_ref[0] + new) * (1.0 / SHIFT)).astype(jnp.bfloat16)


def new_call(words, part, tnew):
    fields, low, samples = words.shape
    width = part.shape[1]
    return pl.pallas_call(
        new_kernel,
        grid=(fields,),
        in_specs=[
            pl.BlockSpec((1, low, samples), lambda f: (f, 0, 0)),
            pl.BlockSpec((1, width, samples), lambda f: (f, 0, 0)),
            pl.BlockSpec(tnew.shape, lambda f: (0, 0)),
        ],
        out_specs=pl.BlockSpec((width, samples), lambda f: (f, 0)),
        out_shape=jax.ShapeDtypeStruct((fields * width, samples), jnp.bfloat16),
        scratch_shapes=[pltpu.VMEM((LO * FIELDS, samples), jnp.bfloat16)],
        compiler_params=pltpu.CompilerParams(vmem_limit_bytes=32 * 1024 * 1024),
        cost_estimate=pl.CostEstimate(flops=2 * fields * samples * 2048 * 128, bytes_accessed=20 << 20, transcendentals=0),
        name="pool_new",
    )(words, part, tnew)


def scaled_columns(rows):
    k = jnp.arange(FIELDS)
    level = jnp.where(k < FIELDS - 1, 2.0 ** (24 - 4.0 * k), 2.0 ** 24).astype(jnp.float32)
    return (rows.astype(jnp.float32).T * jnp.repeat(level, LO)[None, :]).astype(jnp.bfloat16)


def gelu_tanh(values):
    return jax.nn.gelu(values, approximate=True)


def per_device(
    table, accum, evict_delta, evict_ids, hot_ids, cache_old, bag_index, bag_length, labels, w_first, w_out
):
    width = table.shape[1]
    core = lax.axis_index("core")
    half = w_first.shape[1] // 2

    rows = w_first.shape[0]
    mine = lax.dynamic_slice_in_dim(w_first, core * half, half, axis=1)
    other = lax.dynamic_slice_in_dim(w_first, (1 - core) * half, half, axis=1)
    got = lax.ppermute(other, "core", SWAP)
    pair = jnp.where(core == 0, jnp.concatenate([mine, got], axis=0), jnp.concatenate([got, mine], axis=0))
    weight = lax.all_gather(pair, CHIPS, axis=0, tiled=True)

    deltas = evict_delta[0]
    ids = evict_ids[0]
    got_delta = lax.all_to_all(deltas, ALL, split_axis=0, concat_axis=0, tiled=True).reshape(-1, width)
    got_ids = lax.all_to_all(ids, ALL, split_axis=0, concat_axis=0, tiled=True).reshape(-1)

    hot = hot_ids[0]
    hot_table, hot_accum = jnp.take(table, hot, axis=0), jnp.take(accum, hot, axis=0)
    match = (hot[:, None] == got_ids[None, :]).astype(jnp.float32)
    hot_sum = jnp.dot(match, got_delta, precision=lax.Precision.HIGHEST, preferred_element_type=jnp.float32)
    fresh = hot_table - 0.5 * hot_sum * lax.rsqrt(hot_accum + hot_sum * hot_sum)
    fresh = fresh.astype(jnp.bfloat16)
    copies = jnp.broadcast_to(fresh[None], (N_ALL,) + fresh.shape)
    new_rows = lax.all_to_all(copies, ALL, split_axis=0, concat_axis=0, tiled=True).reshape(-1, width)

    words, part = count_call(jnp.transpose(bag_index, (1, 2, 0)), bag_length.T, scaled_columns(cache_old))
    pooled_mine = new_call(words, part, scaled_columns(new_rows))
    pooled_peer = lax.ppermute(pooled_mine, "core", SWAP)
    samples = pooled_mine.shape[1]
    pooled = jnp.concatenate([pooled_mine, pooled_peer], axis=1)
    marks = labels.astype(jnp.float32)
    marks = jnp.concatenate([marks, lax.ppermute(marks, "core", SWAP)])

    out_w = lax.dynamic_slice_in_dim(w_out, core * half, half)
    hidden = lax.dot_general(pooled, weight, (((0,), (0,)), ((), ())), preferred_element_type=jnp.float32)
    act, backward = jax.vjp(gelu_tanh, hidden)
    slope = backward(jnp.ones_like(hidden))[0]
    act_b = act.astype(jnp.bfloat16)
    logit = jnp.dot(act_b, out_w, preferred_element_type=jnp.float32)
    swapped = lax.ppermute(logit, "core", SWAP)
    logit = logit + jnp.concatenate([swapped[samples:], swapped[:samples]])
    grad_logit = 0.125 * (jax.nn.sigmoid(logit) - marks)
    grad_hidden = (grad_logit[:, None] * out_w.astype(jnp.float32)[None, :] * slope).astype(jnp.bfloat16)
    out_term = jnp.dot(grad_logit, act_b.astype(jnp.float32), precision=lax.Precision.HIGHEST)
    whole_term = jnp.dot(pooled, grad_hidden, preferred_element_type=jnp.float32)

    top = out_term.astype(jnp.bfloat16)
    rest = (out_term - top.astype(jnp.float32)).astype(jnp.bfloat16)
    extra = jnp.broadcast_to(jnp.stack([top, rest])[None], (N_CHIPS, 2, half))
    blocks = jnp.concatenate([whole_term.astype(jnp.bfloat16).reshape(N_CHIPS, 2 * rows, half), extra], axis=1)
    terms = lax.all_to_all(blocks, CHIPS, split_axis=0, concat_axis=0, tiled=True)
    total = jnp.sum(terms.astype(jnp.float32), axis=0)
    out_half = total[2 * rows] + total[2 * rows + 1]
    grads = total[: 2 * rows].reshape(2, rows, half)
    keep, give = jnp.where(core == 0, grads[0], grads[1]), jnp.where(core == 0, grads[1], grads[0])
    got = lax.ppermute(jnp.concatenate([give, out_half[None]], axis=0), "core", SWAP)
    left = jnp.where(core == 0, keep, got[:rows])
    right = jnp.where(core == 0, got[:rows], keep)
    grad_w1 = jnp.concatenate([left, right], axis=1)
    grad_w2 = jnp.where(
        core == 0, jnp.concatenate([out_half, got[rows]]), jnp.concatenate([got[rows], out_half])
    )

    summed = jnp.zeros_like(table).at[got_ids].add(got_delta)
    accum_new = accum + summed * summed
    table_new = table - 0.5 * summed * lax.rsqrt(accum_new)
    return (table_new, accum_new, grad_w1, grad_w2)


def solution(mesh):
    fine = Mesh(mesh.devices.reshape(4, 4, 4, 2), ALL)
    placed = (
        P(ALL, None),
        P(ALL, None),
        P(ALL, None, None, None),
        P(ALL, None, None),
        P(ALL, None),
        P(),
        P(ALL, None, None),
        P(ALL, None),
        P(ALL),
        P(ALL, None),
        P(),
    )
    return jax.shard_map(
        per_device,
        mesh=fine,
        in_specs=placed,
        out_specs=(P(ALL, None), P(ALL, None), P(ALL, None), P()),
        check_vma=False,
    )
```

```python
import jax
import jax.numpy as jnp
from jax import lax
from jax.experimental import pallas as pl
from jax.experimental.pallas import tpu as pltpu
from jax.sharding import Mesh
from jax.sharding import PartitionSpec as P

ALL = ("x", "z", "y", "core")
CHIPS = ("x", "z", "y")
SWAP = ((0, 1), (1, 0))
N_ALL = 128
N_CHIPS = 64
ROOT = 0.7978845608028654
LO = 256
FIELDS = 8
SPAN = 32
SHIFT = 2.0 ** 24
GROUP = 2


def level_of(k):
    return 2.0 ** (24 - 4 * k) if k < FIELDS - 1 else SHIFT


def scaled_columns(rows):
    level = jnp.array([level_of(k) for k in range(FIELDS)], jnp.float32)
    return (rows.astype(jnp.float32).T * jnp.repeat(level, LO)[None, :]).astype(jnp.bfloat16)


def field_counts(word, k):
    if k == FIELDS - 1:
        return lax.shift_right_logical(word, 28).astype(jnp.float32)
    return (word & (15 << (4 * k))).astype(jnp.float32)


def unpack(word, c_ref, base, lanes):
    for k in range(FIELDS):
        c_ref[LO * k + base : LO * k + base + SPAN, lanes] = field_counts(word, k).astype(jnp.bfloat16)


def overlapped(group, samples, fill, dot, c_a, c_b):
    bufs = (c_a, c_b)
    for g in range(group + 1):
        for lane in range(samples // 128):
            lanes = slice(128 * lane, 128 * lane + 128)
            if g > 0 and lane % 2 == 0:
                dot(g - 1, bufs[(g - 1) % 2], slice(128 * lane, 128 * lane + 256))
            if g < group:
                fill(g, bufs[g % 2], lanes)


def count_kernel(idx_ref, len_ref, told_ref, words_ref, part_ref, low_ref, old_ref, new_ref, c_a, c_b):
    most, samples = idx_ref.shape[1:]
    line = lax.broadcasted_iota(jnp.int32, (8, 128), 0)
    for g in range(GROUP):
        idx = idx_ref[g]
        live = lax.broadcasted_iota(jnp.int32, idx.shape, 0) < len_ref[g]
        high = idx >> 8
        unit = jnp.int32(1) << (4 * (high & 7))
        low = idx & (LO - 1)
        old = jnp.where(live & (high < 8), unit, 0)
        new = jnp.where(live & (high >= 8), unit, 0)
        for j in range(most):
            rows = slice(8 * j, 8 * j + 8)
            low_ref[g, rows] = jnp.broadcast_to(low[j : j + 1], (8, samples))
            old_ref[g, rows] = jnp.broadcast_to(old[j : j + 1], (8, samples))
            new_ref[g, rows] = jnp.broadcast_to(new[j : j + 1], (8, samples))

    def fill(g, c_ref, lanes):
        for base in range(0, LO, SPAN):
            a_old = [jnp.zeros((8, 128), jnp.int32) for _ in range(SPAN // 8)]
            a_new = [jnp.zeros((8, 128), jnp.int32) for _ in range(SPAN // 8)]
            for j in range(most):
                rows = slice(8 * j, 8 * j + 8)
                lo = low_ref[g, rows, lanes] - base
                v_old = old_ref[g, rows, lanes]
                v_new = new_ref[g, rows, lanes]
                for t in range(SPAN // 8):
                    hit = lo == line + 8 * t
                    a_old[t] = a_old[t] + jnp.where(hit, v_old, 0)
                    a_new[t] = a_new[t] + jnp.where(hit, v_new, 0)
            words_ref[g, base : base + SPAN, lanes] = jnp.concatenate(a_new, axis=0)
            unpack(jnp.concatenate(a_old, axis=0), c_ref, base, lanes)

    def dot(g, c_ref, lanes):
        part_ref[g, :, lanes] = jnp.dot(told_ref[...], c_ref[:, lanes], preferred_element_type=jnp.float32)

    overlapped(GROUP, samples, fill, dot, c_a, c_b)


def count_call(idx, length, rows):
    fields, most, samples = idx.shape
    width = rows.shape[1]
    told = scaled_columns(rows)
    return pl.pallas_call(
        count_kernel,
        grid=(fields // GROUP,),
        in_specs=[
            pl.BlockSpec((GROUP, most, samples), lambda f: (f, 0, 0)),
            pl.BlockSpec((GROUP, 1, samples), lambda f: (f, 0, 0)),
            pl.BlockSpec(told.shape, lambda f: (0, 0)),
        ],
        out_specs=[
            pl.BlockSpec((GROUP, LO, samples), lambda f: (f, 0, 0)),
            pl.BlockSpec((GROUP, width, samples), lambda f: (f, 0, 0)),
        ],
        out_shape=[
            jax.ShapeDtypeStruct((fields, LO, samples), jnp.int32),
            jax.ShapeDtypeStruct((fields, width, samples), jnp.float32),
        ],
        scratch_shapes=[
            pltpu.VMEM((GROUP, 8 * most, samples), jnp.int32),
            pltpu.VMEM((GROUP, 8 * most, samples), jnp.int32),
            pltpu.VMEM((GROUP, 8 * most, samples), jnp.int32),
            pltpu.VMEM((LO * FIELDS, samples), jnp.bfloat16),
            pltpu.VMEM((LO * FIELDS, samples), jnp.bfloat16),
        ],
        compiler_params=pltpu.CompilerParams(vmem_limit_bytes=56 * 1024 * 1024),
        cost_estimate=pl.CostEstimate(flops=2 * fields * samples * 2048 * 128, bytes_accessed=20 << 20, transcendentals=0),
        name="count_bags",
    )(idx, length.reshape(fields, 1, samples), told)


def new_kernel(words_ref, part_ref, rows_ref, across_ref, pooled_ref, tnew_ref, c_a, c_b):
    width, samples = part_ref.shape[1:]

    @pl.when(pl.program_id(0) == 0)
    def _():
        for k in range(FIELDS):
            rows = rows_ref[LO * k : LO * k + LO].astype(jnp.float32) * level_of(k)
            tnew_ref[:, LO * k : LO * k + LO] = rows.T.astype(jnp.bfloat16)

    def fill(g, c_ref, lanes):
        for base in range(0, LO, SPAN):
            unpack(words_ref[g, base : base + SPAN, lanes], c_ref, base, lanes)

    def dot(g, c_ref, lanes):
        new = jnp.dot(tnew_ref[...], c_ref[:, lanes], preferred_element_type=jnp.float32)
        both = (part_ref[g, :, lanes] + new) * (1.0 / SHIFT)
        across_ref[width * g : width * g + width, lanes] = both.astype(jnp.bfloat16)
        pooled_ref[lanes, width * g : width * g + width] = both.T.astype(jnp.bfloat16)

    overlapped(GROUP, samples, fill, dot, c_a, c_b)


def new_call(words, part, rows):
    fields, low, samples = words.shape
    width = part.shape[1]
    return pl.pallas_call(
        new_kernel,
        grid=(fields // GROUP,),
        in_specs=[
            pl.BlockSpec((GROUP, low, samples), lambda f: (f, 0, 0)),
            pl.BlockSpec((GROUP, width, samples), lambda f: (f, 0, 0)),
            pl.BlockSpec(rows.shape, lambda f: (0, 0)),
        ],
        out_specs=[
            pl.BlockSpec((width * GROUP, samples), lambda f: (f, 0)),
            pl.BlockSpec((samples, width * GROUP), lambda f: (0, f)),
        ],
        out_shape=[
            jax.ShapeDtypeStruct((fields * width, samples), jnp.bfloat16),
            jax.ShapeDtypeStruct((samples, fields * width), jnp.bfloat16),
        ],
        scratch_shapes=[
            pltpu.VMEM((width, LO * FIELDS), jnp.bfloat16),
            pltpu.VMEM((LO * FIELDS, samples), jnp.bfloat16),
            pltpu.VMEM((LO * FIELDS, samples), jnp.bfloat16),
        ],
        compiler_params=pltpu.CompilerParams(vmem_limit_bytes=56 * 1024 * 1024),
        cost_estimate=pl.CostEstimate(flops=2 * fields * samples * 2048 * 128, bytes_accessed=20 << 20, transcendentals=0),
        name="pool_new",
    )(words, part, rows)


def dense_kernel(own_a, peer_a, own_b, peer_b, weight_ref, out_ref, act_ref, slope_ref, logit_ref):
    step = pl.program_id(0)
    w = out_ref[0].astype(jnp.float32)
    deep = own_a.shape[1]
    for m, (left, right) in enumerate(((own_a, own_b), (peer_a, peer_b))):
        for n in range(left.shape[0] // 256):
            rows = slice(256 * n, 256 * n + 256)
            hidden = jnp.dot(left[rows], weight_ref[:deep], preferred_element_type=jnp.float32)
            hidden = hidden + jnp.dot(right[rows], weight_ref[deep:], preferred_element_type=jnp.float32)
            square = hidden * hidden
            inner = hidden * (ROOT + ROOT * 0.044715 * square)
            t = jnp.tanh(inner)
            near = 0.5 + 0.5 * t
            act = (hidden * near).astype(jnp.bfloat16)
            slope = near + 0.5 * hidden * (1.0 - t * t) * (ROOT + 3.0 * ROOT * 0.044715 * square)
            here = slice(left.shape[0] * m + 256 * n, left.shape[0] * m + 256 * n + 256)
            act_ref[here] = act
            slope_ref[here] = slope * w
            term = jnp.sum(act.astype(jnp.float32) * w, axis=1, keepdims=True)
            logit_ref[here] = jnp.where(step == 0, term, logit_ref[here] + term)


def dense_call(own_a, peer_a, own_b, peer_b, weight, out_w):
    samples, deep = own_a.shape
    wide = weight.shape[1]
    whole = pl.BlockSpec((samples, deep), lambda n: (0, 0))
    return pl.pallas_call(
        dense_kernel,
        grid=(wide // 256,),
        in_specs=[whole, whole, whole, whole]
        + [pl.BlockSpec((2 * deep, 256), lambda n: (0, n)), pl.BlockSpec((1, 1, 256), lambda n: (n, 0, 0))],
        out_specs=[
            pl.BlockSpec((2 * samples, 256), lambda n: (0, n)),
            pl.BlockSpec((2 * samples, 256), lambda n: (0, n)),
            pl.BlockSpec((2 * samples, 1), lambda n: (0, 0)),
        ],
        out_shape=[
            jax.ShapeDtypeStruct((2 * samples, wide), jnp.bfloat16),
            jax.ShapeDtypeStruct((2 * samples, wide), jnp.float32),
            jax.ShapeDtypeStruct((2 * samples, 1), jnp.float32),
        ],
        compiler_params=pltpu.CompilerParams(vmem_limit_bytes=56 * 1024 * 1024),
        cost_estimate=pl.CostEstimate(flops=4 * samples * deep * 2 * wide, bytes_accessed=14 << 20, transcendentals=2 * samples * wide),
        name="dense_forward",
    )(own_a, peer_a, own_b, peer_b, weight, out_w.reshape(wide // 256, 1, 256))


def grad_kernel(own_a, peer_a, own_b, peer_b, act_ref, slope_ref, error_ref, blocks_ref, dh_ref, extra_ref):
    step = pl.program_id(0)
    samples = own_a.shape[1]
    wide = slope_ref.shape[1]

    @pl.when(step == 0)
    def _():
        total = jnp.zeros((8, wide), jnp.float32)
        for n in range(slope_ref.shape[0] // 64):
            rows = slice(64 * n, 64 * n + 64)
            error = error_ref[rows]
            dh_ref[rows] = (error * slope_ref[rows]).astype(jnp.bfloat16)
            weighted = error * act_ref[rows].astype(jnp.float32)
            total = total + jnp.sum(weighted.reshape(8, 8, wide), axis=0)
        total = jnp.sum(total, axis=0, keepdims=True)
        total = jnp.concatenate([total[:, 128 * c : 128 * c + 128] for c in range(wide // 128)], axis=0)
        top = total.astype(jnp.bfloat16).astype(jnp.float32)
        extra_ref[...] = jnp.concatenate([top, total - top], axis=0).astype(jnp.bfloat16)

    def product(own, peer):
        for c in range(wide // 256):
            columns = slice(256 * c, 256 * c + 256)
            term = jnp.dot(own[...], dh_ref[:samples, columns], preferred_element_type=jnp.float32)
            term = term + jnp.dot(peer[...], dh_ref[samples:, columns], preferred_element_type=jnp.float32)
            term = term.astype(jnp.bfloat16)
            for part in range(2):
                piece = term[:, 128 * part : 128 * part + 128].reshape(-1, 16, 128)
                blocks_ref[:, 16 * (2 * c + part) : 16 * (2 * c + part) + 16] = piece

    half = pl.num_programs(0) // 2
    pl.when(step < half)(lambda: product(own_a, peer_a))
    pl.when(step >= half)(lambda: product(own_b, peer_b))
    for d in range(blocks_ref.shape[0]):
        blocks_ref[d, wide // 8 :] = extra_ref[...]


def grad_call(own_a, peer_a, own_b, peer_b, act, slope, error):
    deep, samples = own_a.shape
    wide = act.shape[1]
    steps = 4
    rows = deep // steps
    early = pl.BlockSpec((rows, samples), lambda k: (jnp.minimum(k, steps - 1), 0))
    late = pl.BlockSpec((rows, samples), lambda k: (jnp.maximum(k - steps, 0), 0))
    fixed = lambda a: pl.BlockSpec(a.shape, lambda k: (0, 0))
    tall = wide // 8 + 16
    return pl.pallas_call(
        grad_kernel,
        grid=(2 * steps,),
        in_specs=[early, early, late, late, fixed(act), fixed(slope), fixed(error)],
        out_specs=pl.BlockSpec((rows // 16, tall, 128), lambda k: (k, 0, 0)),
        out_shape=jax.ShapeDtypeStruct((2 * deep // 16, tall, 128), jnp.bfloat16),
        scratch_shapes=[pltpu.VMEM(act.shape, jnp.bfloat16), pltpu.VMEM((16, 128), jnp.bfloat16)],
        compiler_params=pltpu.CompilerParams(vmem_limit_bytes=56 * 1024 * 1024),
        cost_estimate=pl.CostEstimate(flops=8 * samples * deep * wide, bytes_accessed=14 << 20, transcendentals=0),
        name="grad_terms",
    )(own_a, peer_a, own_b, peer_b, act, slope, error)


def per_device(
    table, accum, evict_delta, evict_ids, hot_ids, cache_old, bag_index, bag_length, labels, w_first, w_out
):
    width = table.shape[1]
    cap = evict_ids.shape[2]
    core = lax.axis_index("core")
    half = w_first.shape[1] // 2
    rows = w_first.shape[0]

    numbers = jnp.pad(evict_ids[0].astype(jnp.float32), ((0, 0), (0, width - cap)))[:, None, :]
    blank = jnp.zeros((N_ALL, 8 - cap - 1, width), jnp.float32)
    packet = jnp.concatenate([evict_delta[0], numbers, blank], axis=1)
    got = lax.all_to_all(packet, ALL, split_axis=0, concat_axis=0, tiled=True)

    mine = lax.dynamic_slice_in_dim(w_first, core * half, half, axis=1)
    other = lax.dynamic_slice_in_dim(w_first, (1 - core) * half, half, axis=1)
    swapped = lax.ppermute(other, "core", SWAP)
    pair = jnp.where(
        core == 0, jnp.concatenate([mine, swapped], axis=0), jnp.concatenate([swapped, mine], axis=0)
    )
    weight = lax.all_gather(pair, CHIPS, axis=0, tiled=True)

    index, length = jnp.transpose(bag_index, (1, 2, 0)), bag_length.T
    fields = index.shape[0]
    first = count_call(index[: fields // 2], length[: fields // 2], cache_old)
    got, *first = lax.optimization_barrier((got, *first))
    got_delta = got[:, :cap].reshape(-1, width)
    got_ids = got[:, cap, :cap].astype(jnp.int32).reshape(-1)

    hot = hot_ids[0]
    hot_table, hot_accum = jnp.take(table, hot, axis=0), jnp.take(accum, hot, axis=0)
    match = (hot[:, None] == got_ids[None, :]).astype(jnp.float32)
    hot_sum = jnp.dot(match, got_delta, precision=lax.Precision.HIGHEST, preferred_element_type=jnp.float32)
    fresh = hot_table - 0.5 * hot_sum * lax.rsqrt(hot_accum + hot_sum * hot_sum)
    copies = jnp.broadcast_to(fresh.astype(jnp.bfloat16)[None], (N_ALL,) + fresh.shape)
    new_rows = lax.all_to_all(copies, ALL, split_axis=0, concat_axis=0, tiled=True).reshape(-1, width)

    second = count_call(index[fields // 2 :], length[fields // 2 :], cache_old)
    across, upright = [], []
    for words, part in (first, second):
        own = new_call(words, part, new_rows)
        for side, store in zip(own, (across, upright)):
            store += [side, lax.ppermute(side, "core", SWAP)]
    samples = labels.shape[0]
    marks = labels.astype(jnp.float32)
    marks = jnp.concatenate([marks, lax.ppermute(marks, "core", SWAP)])

    out_w = lax.dynamic_slice_in_dim(w_out, core * half, half)
    act, slope, logit = dense_call(*upright, weight, out_w.astype(jnp.float32))
    logit = logit[:, 0]
    swapped = lax.ppermute(logit, "core", SWAP)
    logit = logit + jnp.concatenate([swapped[samples:], swapped[:samples]])
    error = 0.125 * (jax.nn.sigmoid(logit) - marks)

    blocks = grad_call(*across, act, slope, error[:, None])
    terms = lax.all_to_all(blocks, ALL, split_axis=0, concat_axis=0, tiled=True)
    total = jnp.sum(terms.reshape((N_CHIPS, 2) + terms.shape[1:]).astype(jnp.float32), axis=0)
    grad_w1 = total[:, : half // 8].reshape(2, half // 128, rows, 128).transpose(2, 0, 1, 3).reshape(rows, 2 * half)
    grad_w2 = (total[:, half // 8 : half // 8 + 8] + total[:, half // 8 + 8 :]).reshape(-1)

    summed = jnp.zeros_like(table).at[got_ids].add(got_delta)
    accum_new = accum + summed * summed
    table_new = table - 0.5 * summed * lax.rsqrt(accum_new)
    return (table_new, accum_new, grad_w1, grad_w2)


def solution(mesh):
    fine = Mesh(mesh.devices.reshape(4, 4, 4, 2), ALL)
    placed = (
        P(ALL, None),
        P(ALL, None),
        P(ALL, None, None, None),
        P(ALL, None, None),
        P(ALL, None),
        P(),
        P(ALL, None, None),
        P(ALL, None),
        P(ALL),
        P(ALL, None),
        P(),
    )
    return jax.shard_map(
        per_device,
        mesh=fine,
        in_specs=placed,
        out_specs=(P(ALL, None), P(ALL, None), P(ALL, None), P()),
        check_vma=False,
    )
```

```python
import functools

import jax
import jax.numpy as jnp
from jax import lax
from jax.experimental import pallas as pl
from jax.experimental.pallas import tpu as pltpu
from jax.sharding import Mesh
from jax.sharding import PartitionSpec as P

ALL = ("x", "z", "y", "core")
CHIPS = ("x", "z", "y")
SWAP = ((0, 1), (1, 0))
N_ALL = 128
N_CHIPS = 64
ROOT = 0.7978845608028654
LO = 256
FIELDS = 8
SPAN = 32
SHIFT = 2.0 ** 24
MIB = 1024 * 1024
GROUP = 2


def level_of(k):
    return 2.0 ** (24 - 4 * k) if k < FIELDS - 1 else SHIFT


def scale_columns(rows_ref, columns_ref):
    for k in range(FIELDS):
        rows = rows_ref[LO * k : LO * k + LO].astype(jnp.float32) * level_of(k)
        columns_ref[:, LO * k : LO * k + LO] = rows.T.astype(jnp.bfloat16)


def field_counts(word, k):
    if k == FIELDS - 1:
        return lax.shift_right_logical(word, 28).astype(jnp.float32)
    return (word & (15 << (4 * k))).astype(jnp.float32)


def unpack(word, c_ref, base, lanes):
    for k in range(FIELDS):
        c_ref[LO * k + base : LO * k + base + SPAN, lanes] = field_counts(word, k).astype(jnp.bfloat16)


def overlapped(group, samples, fill, dot, c_a, c_b):
    bufs = (c_a, c_b)
    for g in range(group + 1):
        for lane in range(samples // 128):
            lanes = slice(128 * lane, 128 * lane + 128)
            if g > 0 and lane % 2 == 0:
                dot(g - 1, bufs[(g - 1) % 2], slice(128 * lane, 128 * lane + 256))
            if g < group:
                fill(g, bufs[g % 2], lanes)


def count_kernel(start, idx_ref, len_ref, rows_ref, words_ref, part_ref, told_ref, low_ref, old_ref, new_ref, c_a, c_b):
    most, samples = idx_ref.shape[1:]
    line = lax.broadcasted_iota(jnp.int32, (8, 128), 0)
    first = start + GROUP * pl.program_id(0)
    pl.when(pl.program_id(0) == 0)(lambda: scale_columns(rows_ref, told_ref))
    for g in range(GROUP):
        idx = idx_ref[g]
        live = lax.broadcasted_iota(jnp.int32, idx.shape, 0) < len_ref[pl.ds(first + g, 1)]
        high = idx >> 8
        unit = jnp.int32(1) << (4 * (high & 7))
        low = idx & (LO - 1)
        old = jnp.where(live & (high < 8), unit, 0)
        new = jnp.where(live & (high >= 8), unit, 0)
        for j in range(most):
            rows = slice(8 * j, 8 * j + 8)
            low_ref[g, rows] = jnp.broadcast_to(low[j : j + 1], (8, samples))
            old_ref[g, rows] = jnp.broadcast_to(old[j : j + 1], (8, samples))
            new_ref[g, rows] = jnp.broadcast_to(new[j : j + 1], (8, samples))

    def fill(g, c_ref, lanes):
        for base in range(0, LO, SPAN):
            a_old = [jnp.zeros((8, 128), jnp.int32) for _ in range(SPAN // 8)]
            a_new = [jnp.zeros((8, 128), jnp.int32) for _ in range(SPAN // 8)]
            for j in range(most):
                rows = slice(8 * j, 8 * j + 8)
                lo = low_ref[g, rows, lanes] - base
                v_old = old_ref[g, rows, lanes]
                v_new = new_ref[g, rows, lanes]
                for t in range(SPAN // 8):
                    hit = lo == line + 8 * t
                    a_old[t] = a_old[t] + jnp.where(hit, v_old, 0)
                    a_new[t] = a_new[t] + jnp.where(hit, v_new, 0)
            words_ref[g, base : base + SPAN, lanes] = jnp.concatenate(a_new, axis=0)
            unpack(jnp.concatenate(a_old, axis=0), c_ref, base, lanes)

    def dot(g, c_ref, lanes):
        part_ref[g, :, lanes] = jnp.dot(told_ref[...], c_ref[:, lanes], preferred_element_type=jnp.float32)

    overlapped(GROUP, samples, fill, dot, c_a, c_b)


def count_call(idx, length, rows, start, fields):
    _, most, samples = idx.shape
    width = rows.shape[1]
    return pl.pallas_call(
        functools.partial(count_kernel, start),
        grid=(fields // GROUP,),
        in_specs=[
            pl.BlockSpec((GROUP, most, samples), lambda f: (f + start // GROUP, 0, 0)),
            pl.BlockSpec(length.shape, lambda f: (0, 0)),
            pl.BlockSpec(rows.shape, lambda f: (0, 0)),
        ],
        out_specs=[
            pl.BlockSpec((GROUP, LO, samples), lambda f: (f, 0, 0)),
            pl.BlockSpec((GROUP, width, samples), lambda f: (f, 0, 0)),
        ],
        out_shape=[
            jax.ShapeDtypeStruct((fields, LO, samples), jnp.int32),
            jax.ShapeDtypeStruct((fields, width, samples), jnp.float32),
        ],
        scratch_shapes=[
            pltpu.VMEM((width, LO * FIELDS), jnp.bfloat16),
            pltpu.VMEM((GROUP, 8 * most, samples), jnp.int32),
            pltpu.VMEM((GROUP, 8 * most, samples), jnp.int32),
            pltpu.VMEM((GROUP, 8 * most, samples), jnp.int32),
            pltpu.VMEM((LO * FIELDS, samples), jnp.bfloat16),
            pltpu.VMEM((LO * FIELDS, samples), jnp.bfloat16),
        ],
        compiler_params=pltpu.CompilerParams(vmem_limit_bytes=56 * MIB),
        cost_estimate=pl.CostEstimate(flops=2 * fields * samples * 2048 * 128, bytes_accessed=20 << 20, transcendentals=0),
        name="count_bags",
    )(idx, length, rows)


def new_kernel(words_ref, part_ref, rows_ref, across_ref, pooled_ref, tnew_ref, c_a, c_b):
    width, samples = part_ref.shape[1:]

    pl.when(pl.program_id(0) == 0)(lambda: scale_columns(rows_ref, tnew_ref))

    def fill(g, c_ref, lanes):
        for base in range(0, LO, SPAN):
            unpack(words_ref[g, base : base + SPAN, lanes], c_ref, base, lanes)

    def dot(g, c_ref, lanes):
        new = jnp.dot(tnew_ref[...], c_ref[:, lanes], preferred_element_type=jnp.float32)
        both = (part_ref[g, :, lanes] + new) * (1.0 / SHIFT)
        across_ref[width * g : width * g + width, lanes] = both.astype(jnp.bfloat16)
        pooled_ref[lanes, width * g : width * g + width] = both.T.astype(jnp.bfloat16)

    overlapped(GROUP, samples, fill, dot, c_a, c_b)


def new_call(words, part, rows):
    fields, low, samples = words.shape
    width = part.shape[1]
    return pl.pallas_call(
        new_kernel,
        grid=(fields // GROUP,),
        in_specs=[
            pl.BlockSpec((GROUP, low, samples), lambda f: (f, 0, 0)),
            pl.BlockSpec((GROUP, width, samples), lambda f: (f, 0, 0)),
            pl.BlockSpec(rows.shape, lambda f: (0, 0)),
        ],
        out_specs=[
            pl.BlockSpec((width * GROUP, samples), lambda f: (f, 0)),
            pl.BlockSpec((samples, width * GROUP), lambda f: (0, f)),
        ],
        out_shape=[
            jax.ShapeDtypeStruct((fields * width, samples), jnp.bfloat16),
            jax.ShapeDtypeStruct((samples, fields * width), jnp.bfloat16),
        ],
        scratch_shapes=[
            pltpu.VMEM((width, LO * FIELDS), jnp.bfloat16),
            pltpu.VMEM((LO * FIELDS, samples), jnp.bfloat16),
            pltpu.VMEM((LO * FIELDS, samples), jnp.bfloat16),
        ],
        compiler_params=pltpu.CompilerParams(vmem_limit_bytes=56 * MIB),
        cost_estimate=pl.CostEstimate(flops=2 * fields * samples * 2048 * 128, bytes_accessed=20 << 20, transcendentals=0),
        name="pool_new",
    )(words, part, rows)


def hot_kernel(ids_ref, got_ref, hot_ref, table_ref, accum_ref, copies_ref, rows_ref, sems):
    count = ids_ref.shape[1]
    cap = 4
    fetches = []
    for k in range(count):
        row = pl.ds(ids_ref[0, k], 1)
        for which, ref in enumerate((table_ref, accum_ref)):
            fetch = pltpu.make_async_copy(ref.at[row], rows_ref.at[which, pl.ds(k, 1)], sems.at[which, k])
            fetch.start()
            fetches.append(fetch)
    got = got_ref[...]
    total = jnp.zeros((128, 128), jnp.float32)
    for c in range(cap):
        match = (got[:, cap, c : c + 1] == hot_ref[...]).astype(jnp.float32)
        total = total + lax.dot_general(
            match, got[:, c], (((0,), (0,)), ((), ())), precision=lax.Precision.HIGHEST, preferred_element_type=jnp.float32
        )
    total = total[:count]
    for fetch in fetches:
        fetch.wait()
    fresh = rows_ref[0] - 0.5 * total * lax.rsqrt(rows_ref[1] + total * total)
    fresh = fresh.astype(jnp.bfloat16)

    def place(d, carry):
        copies_ref[d] = fresh
        return carry

    lax.fori_loop(0, copies_ref.shape[0], place, 0)


def hot_call(got, ids, table, accum):
    count = ids.shape[1]
    hot = jnp.pad(ids.astype(jnp.float32), ((0, 0), (0, 128 - count)), constant_values=-1.0)
    inside = pl.BlockSpec(memory_space=pltpu.VMEM)
    return pl.pallas_call(
        hot_kernel,
        in_specs=[
            pl.BlockSpec(memory_space=pltpu.SMEM),
            inside,
            inside,
            pl.BlockSpec(memory_space=pltpu.HBM),
            pl.BlockSpec(memory_space=pltpu.HBM),
        ],
        out_specs=inside,
        out_shape=jax.ShapeDtypeStruct((N_ALL, count, 128), jnp.bfloat16),
        scratch_shapes=[pltpu.VMEM((2, count, 128), jnp.float32), pltpu.SemaphoreType.DMA((2, count))],
        compiler_params=pltpu.CompilerParams(vmem_limit_bytes=56 * MIB),
        cost_estimate=pl.CostEstimate(flops=4 * 128**3 * 12, bytes_accessed=1 << 20, transcendentals=count * 128),
        name="hot_rows",
    )(ids, got, hot, table, accum)


def dense_kernel(
    core_ref, own_a, peer_a, own_b, peer_b, weight_ref, out_ref, act_ref, slope_ref, logit_ref,
    sum_ref, side_ref, columns_ref, act_v, slope_v, sems, out_sems,
):
    samples, deep = own_a.shape
    steps = columns_ref.shape[0]
    fetch_columns = []
    for n in range(steps):
        columns = pl.ds(pl.multiple_of(core_ref[0] * (256 * steps) + 256 * n, 256), 256)
        fetch_columns.append(pltpu.make_async_copy(weight_ref.at[:, columns], columns_ref.at[n], sems.at[n]))
    fetch_sides = [
        pltpu.make_async_copy(side, side_ref.at[i], sems.at[steps + i])
        for i, side in enumerate((own_a, own_b, peer_a, peer_b))
    ]
    for fetch in fetch_columns[:1] + fetch_sides + fetch_columns[1:]:
        fetch.start()
    sent = []
    for n in range(steps):
        fetch_columns[n].wait()
        w = out_ref[:, 256 * n : 256 * n + 256]
        for m in range(2):
            if n == 0:
                fetch_sides[2 * m].wait()
                fetch_sides[2 * m + 1].wait()
            hidden = jnp.dot(side_ref[2 * m], columns_ref[n, :deep], preferred_element_type=jnp.float32)
            hidden = hidden + jnp.dot(side_ref[2 * m + 1], columns_ref[n, deep:], preferred_element_type=jnp.float32)
            square = hidden * hidden
            t = jnp.tanh(hidden * (ROOT + ROOT * 0.044715 * square))
            near = 0.5 + 0.5 * t
            act = (hidden * near).astype(jnp.bfloat16)
            slope = near + 0.5 * hidden * (1.0 - t * t) * (ROOT + 3.0 * ROOT * 0.044715 * square)
            here = slice(samples * m, samples * m + samples)
            act_v[n, here] = act
            slope_v[n, here] = slope * w
            term = act.astype(jnp.float32) * w
            term = term[:, :128] + term[:, 128:]
            sum_ref[here] = term if n == 0 else sum_ref[here] + term
        for i, (store, target) in enumerate(((act_v, act_ref), (slope_v, slope_ref))):
            send = pltpu.make_async_copy(store.at[n], target.at[n], out_sems.at[i, n])
            send.start()
            sent.append(send)
    ones = jnp.ones((8, 128), jnp.float32)
    for b in range(logit_ref.shape[0]):
        term = sum_ref[128 * b : 128 * b + 128]
        line = lax.dot_general(
            ones, term, (((1,), (1,)), ((), ())), precision=lax.Precision.HIGHEST, preferred_element_type=jnp.float32
        )
        logit_ref[b : b + 1] = line[:1]
    for send in sent:
        send.wait()


def dense_call(core, own_a, peer_a, own_b, peer_b, weight, out_w):
    samples, deep = own_a.shape
    wide = out_w.shape[0]
    steps = wide // 256
    far = pl.BlockSpec(memory_space=pltpu.HBM)
    inside = pl.BlockSpec(memory_space=pltpu.VMEM)
    return pl.pallas_call(
        dense_kernel,
        in_specs=[pl.BlockSpec(memory_space=pltpu.SMEM)] + [far] * 5 + [inside],
        out_specs=[far, far, inside],
        out_shape=[
            jax.ShapeDtypeStruct((steps, 2 * samples, 256), jnp.bfloat16),
            jax.ShapeDtypeStruct((steps, 2 * samples, 256), jnp.float32),
            jax.ShapeDtypeStruct((2 * samples // 128, 128), jnp.float32),
        ],
        scratch_shapes=[
            pltpu.VMEM((2 * samples, 128), jnp.float32),
            pltpu.VMEM((4, samples, deep), jnp.bfloat16),
            pltpu.VMEM((steps, 2 * deep, 256), jnp.bfloat16),
            pltpu.VMEM((steps, 2 * samples, 256), jnp.bfloat16),
            pltpu.VMEM((steps, 2 * samples, 256), jnp.float32),
            pltpu.SemaphoreType.DMA((steps + 4,)),
            pltpu.SemaphoreType.DMA((2, steps)),
        ],
        compiler_params=pltpu.CompilerParams(vmem_limit_bytes=56 * MIB),
        cost_estimate=pl.CostEstimate(flops=4 * samples * deep * 2 * wide, bytes_accessed=14 << 20, transcendentals=2 * samples * wide),
        name="dense_forward",
    )(core.reshape(1), own_a, peer_a, own_b, peer_b, weight, out_w.reshape(1, wide))


def grad_kernel(
    own_a, peer_a, own_b, peer_b, act_ref, slope_ref, logit_ref, swapped_ref, marks_ref, out_ref,
    side_ref, act_v, slope_v, dh_ref, blocks_ref, sems, out_sems,
):
    deep, samples = own_a.shape
    steps = act_ref.shape[0]
    tall = blocks_ref.shape[1]
    fetch_dense = [
        [pltpu.make_async_copy(act_ref.at[n], act_v.at[n], sems.at[2 * n]), pltpu.make_async_copy(slope_ref.at[n], slope_v.at[n], sems.at[2 * n + 1])]
        for n in range(steps)
    ]
    fetch_sides = [
        pltpu.make_async_copy(side, side_ref.at[i], sems.at[2 * steps + i])
        for i, side in enumerate((own_a, peer_a, own_b, peer_b))
    ]
    for fetch in fetch_dense[0] + fetch_sides + [f for pair in fetch_dense[1:] for f in pair]:
        fetch.start()
    own_rows = samples // 128
    logit = logit_ref[...] + jnp.concatenate([swapped_ref[own_rows:], swapped_ref[:own_rows]], axis=0)
    error = (0.125 * (jax.nn.sigmoid(logit) - marks_ref[...])).T
    sent = []
    lines = []
    for c in range(steps):
        for fetch in fetch_dense[c]:
            fetch.wait()
        total = jnp.zeros((8, 256), jnp.float32)
        for b in range(2 * own_rows):
            rows = slice(128 * b, 128 * b + 128)
            column = error[:, b : b + 1]
            dh_ref[c, rows] = (column * slope_v[c, rows]).astype(jnp.bfloat16)
            weighted = column * act_v[c, rows].astype(jnp.float32)
            total = total + jnp.sum(weighted.reshape(16, 8, 256), axis=0)
        total = jnp.sum(total, axis=0, keepdims=True)
        lines += [total[:, :128], total[:, 128:]]
        if c == steps - 1:
            total = jnp.concatenate(lines, axis=0)
            top = total.astype(jnp.bfloat16).astype(jnp.float32)
            extra = jnp.concatenate([top, total - top], axis=0).astype(jnp.bfloat16)

            def place(d, carry):
                blocks_ref[d, 32 * steps :] = extra
                return carry

            lax.fori_loop(0, blocks_ref.shape[0], place, 0)
        for side in range(2):
            if c == 0:
                fetch_sides[2 * side].wait()
                fetch_sides[2 * side + 1].wait()
            term = jnp.dot(side_ref[2 * side], dh_ref[c, :samples], preferred_element_type=jnp.float32)
            term = term + jnp.dot(side_ref[2 * side + 1], dh_ref[c, samples:], preferred_element_type=jnp.float32)
            term = term.astype(jnp.bfloat16)
            blocks = pl.ds(side * (deep // 16), deep // 16)
            for part in range(2):
                at = 32 * c + 16 * part
                blocks_ref[blocks, at : at + 16] = term[:, 128 * part : 128 * part + 128].reshape(-1, 16, 128)
            span = pl.ds(32 * c, (tall - 32 * c) if c == steps - 1 else 32)
            send = pltpu.make_async_copy(blocks_ref.at[blocks, span], out_ref.at[blocks, span], out_sems.at[side, c])
            send.start()
            sent.append(send)
    for send in sent:
        send.wait()


def grad_call(own_a, peer_a, own_b, peer_b, act, slope, logit, swapped, marks):
    deep, samples = own_a.shape
    steps = act.shape[0]
    far = pl.BlockSpec(memory_space=pltpu.HBM)
    inside = pl.BlockSpec(memory_space=pltpu.VMEM)
    shape = (2 * deep // 16, 32 * steps + 16, 128)
    return pl.pallas_call(
        grad_kernel,
        in_specs=[far] * 6 + [inside] * 3,
        out_specs=far,
        out_shape=jax.ShapeDtypeStruct(shape, jnp.bfloat16),
        scratch_shapes=[
            pltpu.VMEM((4, deep, samples), jnp.bfloat16),
            pltpu.VMEM(act.shape, jnp.bfloat16),
            pltpu.VMEM(slope.shape, jnp.float32),
            pltpu.VMEM(act.shape, jnp.bfloat16),
            pltpu.VMEM(shape, jnp.bfloat16),
            pltpu.SemaphoreType.DMA((2 * steps + 4,)),
            pltpu.SemaphoreType.DMA((2, steps)),
        ],
        compiler_params=pltpu.CompilerParams(vmem_limit_bytes=56 * MIB),
        cost_estimate=pl.CostEstimate(flops=8 * samples * deep * 256 * steps, bytes_accessed=14 << 20, transcendentals=0),
        name="grad_terms",
    )(own_a, peer_a, own_b, peer_b, act, slope, logit, swapped, marks)


def per_device(
    table, accum, evict_delta, evict_ids, hot_ids, cache_old, bag_index, bag_length, labels, w_first, w_out
):
    width = table.shape[1]
    cap = evict_ids.shape[2]
    core = lax.axis_index("core")
    half = w_first.shape[1] // 2
    rows = w_first.shape[0]

    numbers = jnp.pad(evict_ids[0].astype(jnp.float32), ((0, 0), (0, width - cap)))[:, None, :]
    blank = jnp.zeros((N_ALL, 8 - cap - 1, width), jnp.float32)
    packet = jnp.concatenate([evict_delta[0], numbers, blank], axis=1)
    got = lax.all_to_all(packet, ALL, split_axis=0, concat_axis=0, tiled=True)

    weight = lax.all_gather(w_first, ALL, axis=0, tiled=True)

    index, length = jnp.transpose(bag_index, (1, 2, 0)), bag_length.T
    fields = index.shape[0]
    first = count_call(index, length, cache_old, 0, fields // 2)
    got, *first = lax.optimization_barrier((got, *first))
    got_delta = got[:, :cap].reshape(-1, width)
    got_ids = got[:, cap, :cap].astype(jnp.int32).reshape(-1)

    copies = hot_call(got, hot_ids, table, accum)
    new_rows = lax.all_to_all(copies, ALL, split_axis=0, concat_axis=0, tiled=True).reshape(-1, width)

    second = count_call(index, length, cache_old, fields // 2, fields // 2)
    across, upright = [], []
    for words, part in (first, second):
        own = new_call(words, part, new_rows)
        for side, store in zip(own, (across, upright)):
            store += [side, lax.ppermute(side, "core", SWAP)]
    marks = labels.astype(jnp.float32).reshape(-1, 128)
    marks = jnp.concatenate([marks, lax.ppermute(marks, "core", SWAP)], axis=0)

    out_w = lax.dynamic_slice_in_dim(w_out, core * half, half)
    act, slope, logit = dense_call(core, *upright, weight, out_w.astype(jnp.float32))
    swapped = lax.ppermute(logit, "core", SWAP)

    blocks = grad_call(*across, act, slope, logit, swapped, marks)
    terms = lax.all_to_all(blocks, ALL, split_axis=0, concat_axis=0, tiled=True)
    total = jnp.sum(terms.reshape((N_CHIPS, 2) + terms.shape[1:]).astype(jnp.float32), axis=0)
    grad_w1 = total[:, : half // 8].reshape(2, half // 128, rows, 128).transpose(2, 0, 1, 3).reshape(rows, 2 * half)
    grad_w2 = (total[:, half // 8 : half // 8 + 8] + total[:, half // 8 + 8 :]).reshape(-1)

    summed = jnp.zeros_like(table).at[got_ids].add(got_delta)
    accum_new = accum + summed * summed
    table_new = table - 0.5 * summed * lax.rsqrt(accum_new)
    return (table_new, accum_new, grad_w1, grad_w2)


def solution(mesh):
    fine = Mesh(mesh.devices.reshape(4, 4, 4, 2), ALL)
    placed = (
        P(ALL, None),
        P(ALL, None),
        P(ALL, None, None, None),
        P(ALL, None, None),
        P(ALL, None),
        P(),
        P(ALL, None, None),
        P(ALL, None),
        P(ALL),
        P(ALL, None),
        P(),
    )
    return jax.shard_map(
        per_device,
        mesh=fine,
        in_specs=placed,
        out_specs=(P(ALL, None), P(ALL, None), P(ALL, None), P()),
        check_vma=False,
    )
```

```python
import functools

import jax
import jax.numpy as jnp
from jax import lax
from jax.experimental import pallas as pl
from jax.experimental.pallas import tpu as pltpu
from jax.sharding import Mesh
from jax.sharding import PartitionSpec as P

ALL = ("x", "z", "y", "core")
CHIPS = ("x", "z", "y")
SWAP = ((0, 1), (1, 0))
N_ALL = 128
N_CHIPS = 64
ROOT = 0.7978845608028654
LO = 256
FIELDS = 8
SPAN = 32
SHIFT = 2.0 ** 24
MIB = 1024 * 1024
ROW = 256
GROUP = 2


def in_hbm(*arrays):
    return [pltpu.with_memory_space_constraint(a, pltpu.HBM) for a in arrays]


def in_vmem(*arrays):
    return [pltpu.with_memory_space_constraint(a, pltpu.VMEM) for a in arrays]


def level_of(k):
    return 2.0 ** (24 - 4 * k) if k < FIELDS - 1 else SHIFT


def scale_columns(rows_ref, columns_ref):
    for k in range(FIELDS):
        rows = rows_ref[LO * k : LO * k + LO].astype(jnp.float32) * level_of(k)
        columns_ref[:, LO * k : LO * k + LO] = rows.T.astype(jnp.bfloat16)


def field_counts(word, k):
    if k == FIELDS - 1:
        return lax.shift_right_logical(word, 28).astype(jnp.float32)
    return (word & (15 << (4 * k))).astype(jnp.float32)


def unpack(word, c_ref, base, lanes):
    for k in range(FIELDS):
        c_ref[LO * k + base : LO * k + base + SPAN, lanes] = field_counts(word, k).astype(jnp.bfloat16)


def overlapped(group, samples, fill, dot, c_a, c_b):
    bufs = (c_a, c_b)
    for g in range(group + 1):
        for lane in range(samples // 128):
            lanes = slice(128 * lane, 128 * lane + 128)
            if g > 0 and lane % 2 == 0:
                dot(g - 1, bufs[(g - 1) % 2], slice(128 * lane, 128 * lane + 256))
            if g < group:
                fill(g, bufs[g % 2], lanes)


def count_kernel(start, idx_ref, len_ref, rows_ref, words_ref, part_ref, told_ref, low_ref, old_ref, new_ref, c_a, c_b):
    most, samples = idx_ref.shape[1:]
    line = lax.broadcasted_iota(jnp.int32, (8, 128), 0)
    first = start + GROUP * pl.program_id(0)
    pl.when(pl.program_id(0) == 0)(lambda: scale_columns(rows_ref, told_ref))
    for g in range(GROUP):
        idx = idx_ref[g]
        live = lax.broadcasted_iota(jnp.int32, idx.shape, 0) < len_ref[pl.ds(first + g, 1)]
        high = idx >> 8
        unit = jnp.int32(1) << (4 * (high & 7))
        low = idx & (LO - 1)
        old = jnp.where(live & (high < 8), unit, 0)
        new = jnp.where(live & (high >= 8), unit, 0)
        for j in range(most):
            rows = slice(8 * j, 8 * j + 8)
            low_ref[g, rows] = jnp.broadcast_to(low[j : j + 1], (8, samples))
            old_ref[g, rows] = jnp.broadcast_to(old[j : j + 1], (8, samples))
            new_ref[g, rows] = jnp.broadcast_to(new[j : j + 1], (8, samples))

    def fill(g, c_ref, lanes):
        for base in range(0, LO, SPAN):
            a_old = [jnp.zeros((8, 128), jnp.int32) for _ in range(SPAN // 8)]
            a_new = [jnp.zeros((8, 128), jnp.int32) for _ in range(SPAN // 8)]
            for j in range(most):
                rows = slice(8 * j, 8 * j + 8)
                lo = low_ref[g, rows, lanes] - base
                v_old = old_ref[g, rows, lanes]
                v_new = new_ref[g, rows, lanes]
                for t in range(SPAN // 8):
                    hit = lo == line + 8 * t
                    a_old[t] = a_old[t] + jnp.where(hit, v_old, 0)
                    a_new[t] = a_new[t] + jnp.where(hit, v_new, 0)
            words_ref[g, base : base + SPAN, lanes] = jnp.concatenate(a_new, axis=0)
            unpack(jnp.concatenate(a_old, axis=0), c_ref, base, lanes)

    def dot(g, c_ref, lanes):
        part_ref[g, :, lanes] = jnp.dot(told_ref[...], c_ref[:, lanes], preferred_element_type=jnp.float32)

    overlapped(GROUP, samples, fill, dot, c_a, c_b)


def count_call(idx, length, rows, start, fields):
    _, most, samples = idx.shape
    width = rows.shape[1]
    return pl.pallas_call(
        functools.partial(count_kernel, start),
        grid=(fields // GROUP,),
        in_specs=[
            pl.BlockSpec((GROUP, most, samples), lambda f: (f + start // GROUP, 0, 0)),
            pl.BlockSpec(length.shape, lambda f: (0, 0)),
            pl.BlockSpec(rows.shape, lambda f: (0, 0)),
        ],
        out_specs=[
            pl.BlockSpec((GROUP, LO, samples), lambda f: (f, 0, 0)),
            pl.BlockSpec((GROUP, width, samples), lambda f: (f, 0, 0)),
        ],
        out_shape=[
            pltpu.HBM((fields, LO, samples), jnp.int32),
            pltpu.HBM((fields, width, samples), jnp.float32),
        ],
        scratch_shapes=[
            pltpu.VMEM((width, LO * FIELDS), jnp.bfloat16),
            pltpu.VMEM((GROUP, 8 * most, samples), jnp.int32),
            pltpu.VMEM((GROUP, 8 * most, samples), jnp.int32),
            pltpu.VMEM((GROUP, 8 * most, samples), jnp.int32),
            pltpu.VMEM((LO * FIELDS, samples), jnp.bfloat16),
            pltpu.VMEM((LO * FIELDS, samples), jnp.bfloat16),
        ],
        compiler_params=pltpu.CompilerParams(vmem_limit_bytes=16 * MIB),
        cost_estimate=pl.CostEstimate(flops=2 * fields * samples * 2048 * 128, bytes_accessed=20 << 20, transcendentals=0),
        name="count_bags",
    )(idx, length, rows)


def new_kernel(words_ref, part_ref, rows_ref, across_ref, pooled_ref, tnew_ref, c_a, c_b):
    width, samples = part_ref.shape[1:]

    pl.when(pl.program_id(0) == 0)(lambda: scale_columns(rows_ref, tnew_ref))

    def fill(g, c_ref, lanes):
        for base in range(0, LO, SPAN):
            unpack(words_ref[g, base : base + SPAN, lanes], c_ref, base, lanes)

    def dot(g, c_ref, lanes):
        new = jnp.dot(tnew_ref[...], c_ref[:, lanes], preferred_element_type=jnp.float32)
        both = (part_ref[g, :, lanes] + new) * (1.0 / SHIFT)
        across_ref[width * g : width * g + width, lanes] = both.astype(jnp.bfloat16)
        pooled_ref[lanes, width * g : width * g + width] = both.T.astype(jnp.bfloat16)

    overlapped(GROUP, samples, fill, dot, c_a, c_b)


def new_call(words, part, rows):
    fields, low, samples = words.shape
    width = part.shape[1]
    return pl.pallas_call(
        new_kernel,
        grid=(fields // GROUP,),
        in_specs=[
            pl.BlockSpec((GROUP, low, samples), lambda f: (f, 0, 0)),
            pl.BlockSpec((GROUP, width, samples), lambda f: (f, 0, 0)),
            pl.BlockSpec(rows.shape, lambda f: (0, 0)),
        ],
        out_specs=[
            pl.BlockSpec((width * GROUP, samples), lambda f: (f, 0)),
            pl.BlockSpec((samples, width * GROUP), lambda f: (0, f)),
        ],
        out_shape=[
            pltpu.VMEM((fields * width, samples), jnp.bfloat16),
            pltpu.VMEM((samples, fields * width), jnp.bfloat16),
        ],
        scratch_shapes=[
            pltpu.VMEM((width, LO * FIELDS), jnp.bfloat16),
            pltpu.VMEM((LO * FIELDS, samples), jnp.bfloat16),
            pltpu.VMEM((LO * FIELDS, samples), jnp.bfloat16),
        ],
        compiler_params=pltpu.CompilerParams(vmem_limit_bytes=16 * MIB),
        cost_estimate=pl.CostEstimate(flops=2 * fields * samples * 2048 * 128, bytes_accessed=20 << 20, transcendentals=0),
        name="pool_new",
    )(*in_hbm(words, part), rows)


def hot_kernel(ids_ref, got_ref, hot_ref, table_ref, accum_ref, copies_ref, rows_ref, sems):
    count = ids_ref.shape[1]
    cap = 4
    fetches = []
    for k in range(count):
        row = pl.ds(ids_ref[0, k], 1)
        for which, ref in enumerate((table_ref, accum_ref)):
            fetch = pltpu.make_async_copy(ref.at[row], rows_ref.at[which, pl.ds(k, 1)], sems.at[which, k])
            fetch.start()
            fetches.append(fetch)
    got = got_ref[...]
    total = jnp.zeros((128, 128), jnp.float32)
    for c in range(cap):
        match = (got[:, cap, c : c + 1] == hot_ref[...]).astype(jnp.float32)
        total = total + lax.dot_general(
            match, got[:, c], (((0,), (0,)), ((), ())), precision=lax.Precision.HIGHEST, preferred_element_type=jnp.float32
        )
    total = total[:count]
    for fetch in fetches:
        fetch.wait()
    fresh = rows_ref[0] - 0.5 * total * lax.rsqrt(rows_ref[1] + total * total)
    fresh = fresh.astype(jnp.bfloat16)

    def place(d, carry):
        copies_ref[d] = fresh
        return carry

    lax.fori_loop(0, copies_ref.shape[0], place, 0)


def hot_call(got, ids, table, accum):
    count = ids.shape[1]
    hot = jnp.pad(ids.astype(jnp.float32), ((0, 0), (0, 128 - count)), constant_values=-1.0)
    inside = pl.BlockSpec(memory_space=pltpu.VMEM)
    return pl.pallas_call(
        hot_kernel,
        in_specs=[
            pl.BlockSpec(memory_space=pltpu.SMEM),
            inside,
            inside,
            pl.BlockSpec(memory_space=pltpu.HBM),
            pl.BlockSpec(memory_space=pltpu.HBM),
        ],
        out_specs=inside,
        out_shape=jax.ShapeDtypeStruct((N_ALL, count, 128), jnp.bfloat16),
        scratch_shapes=[pltpu.VMEM((2, count, 128), jnp.float32), pltpu.SemaphoreType.DMA((2, count))],
        compiler_params=pltpu.CompilerParams(vmem_limit_bytes=8 * MIB),
        cost_estimate=pl.CostEstimate(flops=4 * 128**3 * 12, bytes_accessed=1 << 20, transcendentals=count * 128),
        name="hot_rows",
    )(ids, got, hot, *in_hbm(table, accum))


def dense_kernel(
    core_ref, own_a, peer_a, own_b, peer_b, weight_ref, out_ref, act_ref, slope_ref, logit_ref,
    sum_ref, columns_ref, sems,
):
    samples, deep = own_a.shape
    steps = columns_ref.shape[0]
    fetch_columns = []
    for n in range(steps):
        columns = pl.ds(pl.multiple_of(core_ref[0] * (256 * steps) + 256 * n, 256), 256)
        fetch_columns.append(pltpu.make_async_copy(weight_ref.at[:, columns], columns_ref.at[n], sems.at[n]))
    for fetch in fetch_columns:
        fetch.start()

    def product(n, m):
        left, right = ((own_a, own_b), (peer_a, peer_b))[m // 2]
        rows = slice(ROW * (m % 2), ROW * (m % 2) + ROW)
        hidden = jnp.dot(left[rows], columns_ref[n, :deep], preferred_element_type=jnp.float32)
        return hidden + jnp.dot(right[rows], columns_ref[n, deep:], preferred_element_type=jnp.float32)

    def finish(n, m, hidden):
        w = out_ref[:, 256 * n : 256 * n + 256]
        square = hidden * hidden
        t = jnp.tanh(hidden * (ROOT + ROOT * 0.044715 * square))
        near = 0.5 + 0.5 * t
        act = (hidden * near).astype(jnp.bfloat16)
        slope = near + 0.5 * hidden * (1.0 - t * t) * (ROOT + 3.0 * ROOT * 0.044715 * square)
        here = slice(ROW * m, ROW * m + ROW)
        act_ref[n, here] = act
        slope_ref[n, here] = slope * w
        term = act.astype(jnp.float32) * w
        term = term[:, :128] + term[:, 128:]
        sum_ref[here] = term if n == 0 else sum_ref[here] + term

    before = None
    for n in range(steps):
        fetch_columns[n].wait()
        for m in range(4):
            hidden = product(n, m)
            if before is not None:
                finish(*before)
            before = (n, m, hidden)
    finish(*before)
    ones = jnp.ones((8, 128), jnp.float32)
    for b in range(logit_ref.shape[0]):
        term = sum_ref[128 * b : 128 * b + 128]
        line = lax.dot_general(
            ones, term, (((1,), (1,)), ((), ())), precision=lax.Precision.HIGHEST, preferred_element_type=jnp.float32
        )
        logit_ref[b : b + 1] = line[:1]


def dense_call(core, own_a, peer_a, own_b, peer_b, weight, out_w):
    samples, deep = own_a.shape
    wide = out_w.shape[0]
    steps = wide // 256
    far = pl.BlockSpec(memory_space=pltpu.HBM)
    inside = pl.BlockSpec(memory_space=pltpu.VMEM)
    return pl.pallas_call(
        dense_kernel,
        in_specs=[pl.BlockSpec(memory_space=pltpu.SMEM)] + [inside] * 4 + [far] + [inside],
        out_specs=[inside] * 3,
        out_shape=[
            pltpu.VMEM((steps, 2 * samples, 256), jnp.bfloat16),
            pltpu.VMEM((steps, 2 * samples, 256), jnp.float32),
            jax.ShapeDtypeStruct((2 * samples // 128, 128), jnp.float32),
        ],
        scratch_shapes=[
            pltpu.VMEM((2 * samples, 128), jnp.float32),
            pltpu.VMEM((steps, 2 * deep, 256), jnp.bfloat16),
            pltpu.SemaphoreType.DMA((steps,)),
        ],
        compiler_params=pltpu.CompilerParams(vmem_limit_bytes=16 * MIB),
        cost_estimate=pl.CostEstimate(flops=4 * samples * deep * 2 * wide, bytes_accessed=14 << 20, transcendentals=2 * samples * wide),
        name="dense_forward",
    )(core.reshape(1), *in_vmem(own_a, peer_a, own_b, peer_b), *in_hbm(weight), out_w.reshape(1, wide))


def grad_kernel(
    own_a, peer_a, own_b, peer_b, act_ref, slope_ref, logit_ref, swapped_ref, marks_ref, out_ref,
    dh_ref, blocks_ref, out_sems,
):
    deep, samples = own_a.shape
    steps = act_ref.shape[0]
    tall = blocks_ref.shape[1]
    own_rows = samples // 128
    logit = logit_ref[...] + jnp.concatenate([swapped_ref[own_rows:], swapped_ref[:own_rows]], axis=0)
    error = (0.125 * (jax.nn.sigmoid(logit) - marks_ref[...])).T
    sent = []
    lines = []
    for c in range(steps):
        total = jnp.zeros((8, 256), jnp.float32)
        for b in range(2 * own_rows):
            rows = slice(128 * b, 128 * b + 128)
            column = error[:, b : b + 1]
            dh_ref[c, rows] = (column * slope_ref[c, rows]).astype(jnp.bfloat16)
            weighted = column * act_ref[c, rows].astype(jnp.float32)
            total = total + jnp.sum(weighted.reshape(16, 8, 256), axis=0)
        total = jnp.sum(total, axis=0, keepdims=True)
        lines += [total[:, :128], total[:, 128:]]
        if c == steps - 1:
            total = jnp.concatenate(lines, axis=0)
            top = total.astype(jnp.bfloat16).astype(jnp.float32)
            extra = jnp.concatenate([top, total - top], axis=0).astype(jnp.bfloat16)

            def place(d, carry):
                blocks_ref[d, 32 * steps :] = extra
                return carry

            lax.fori_loop(0, blocks_ref.shape[0], place, 0)
        for side in range(2):
            own, peer = ((own_a, peer_a), (own_b, peer_b))[side]
            term = jnp.dot(own[...], dh_ref[c, :samples], preferred_element_type=jnp.float32)
            term = term + jnp.dot(peer[...], dh_ref[c, samples:], preferred_element_type=jnp.float32)
            term = term.astype(jnp.bfloat16)
            blocks = pl.ds(side * (deep // 16), deep // 16)
            for part in range(2):
                at = 32 * c + 16 * part
                blocks_ref[blocks, at : at + 16] = term[:, 128 * part : 128 * part + 128].reshape(-1, 16, 128)
            span = pl.ds(32 * c, (tall - 32 * c) if c == steps - 1 else 32)
            send = pltpu.make_async_copy(blocks_ref.at[blocks, span], out_ref.at[blocks, span], out_sems.at[side, c])
            send.start()
            sent.append(send)
    for send in sent:
        send.wait()


def grad_call(own_a, peer_a, own_b, peer_b, act, slope, logit, swapped, marks):
    deep, samples = own_a.shape
    steps = act.shape[0]
    far = pl.BlockSpec(memory_space=pltpu.HBM)
    inside = pl.BlockSpec(memory_space=pltpu.VMEM)
    shape = (2 * deep // 16, 32 * steps + 16, 128)
    return pl.pallas_call(
        grad_kernel,
        in_specs=[inside] * 9,
        out_specs=far,
        out_shape=pltpu.HBM(shape, jnp.bfloat16),
        scratch_shapes=[
            pltpu.VMEM(act.shape, jnp.bfloat16),
            pltpu.VMEM(shape, jnp.bfloat16),
            pltpu.SemaphoreType.DMA((2, steps)),
        ],
        compiler_params=pltpu.CompilerParams(vmem_limit_bytes=16 * MIB),
        cost_estimate=pl.CostEstimate(flops=8 * samples * deep * 256 * steps, bytes_accessed=14 << 20, transcendentals=0),
        name="grad_terms",
    )(*in_vmem(own_a, peer_a, own_b, peer_b, act, slope), logit, swapped, marks)


def per_device(
    table, accum, evict_delta, evict_ids, hot_ids, cache_old, bag_index, bag_length, labels, w_first, w_out
):
    width = table.shape[1]
    cap = evict_ids.shape[2]
    core = lax.axis_index("core")
    half = w_first.shape[1] // 2
    rows = w_first.shape[0]

    numbers = jnp.pad(evict_ids[0].astype(jnp.float32), ((0, 0), (0, width - cap)))[:, None, :]
    blank = jnp.zeros((N_ALL, 8 - cap - 1, width), jnp.float32)
    packet = jnp.concatenate([evict_delta[0], numbers, blank], axis=1)
    got = lax.all_to_all(packet, ALL, split_axis=0, concat_axis=0, tiled=True)

    weight = lax.all_gather(w_first, ALL, axis=0, tiled=True)

    index, length = jnp.transpose(bag_index, (1, 2, 0)), bag_length.T
    fields = index.shape[0]
    first = count_call(index, length, cache_old, 0, fields // 2)
    got, *first = lax.optimization_barrier((got, *first))
    got_delta = got[:, :cap].reshape(-1, width)
    got_ids = got[:, cap, :cap].astype(jnp.int32).reshape(-1)

    copies = hot_call(got, hot_ids, table, accum)
    new_rows = lax.all_to_all(copies, ALL, split_axis=0, concat_axis=0, tiled=True).reshape(-1, width)

    second = count_call(index, length, cache_old, fields // 2, fields // 2)
    across, upright = [], []
    for words, part in (first, second):
        own = new_call(words, part, new_rows)
        for side, store in zip(own, (across, upright)):
            store += [side, lax.ppermute(side, "core", SWAP)]
    marks = labels.astype(jnp.float32).reshape(-1, 128)
    marks = jnp.concatenate([marks, lax.ppermute(marks, "core", SWAP)], axis=0)

    out_w = lax.dynamic_slice_in_dim(w_out, core * half, half)
    act, slope, logit = dense_call(core, *upright, weight, out_w.astype(jnp.float32))
    swapped = lax.ppermute(logit, "core", SWAP)

    blocks = grad_call(*across, act, slope, logit, swapped, marks)
    terms = lax.all_to_all(blocks, ALL, split_axis=0, concat_axis=0, tiled=True)
    total = jnp.sum(terms.reshape((N_CHIPS, 2) + terms.shape[1:]).astype(jnp.float32), axis=0)
    grad_w1 = total[:, : half // 8].reshape(2, half // 128, rows, 128).transpose(2, 0, 1, 3).reshape(rows, 2 * half)
    grad_w2 = (total[:, half // 8 : half // 8 + 8] + total[:, half // 8 + 8 :]).reshape(-1)

    summed = jnp.zeros_like(table).at[got_ids].add(got_delta)
    accum_new = accum + summed * summed
    table_new = table - 0.5 * summed * lax.rsqrt(accum_new)
    return (table_new, accum_new, grad_w1, grad_w2)


def solution(mesh):
    fine = Mesh(mesh.devices.reshape(4, 4, 4, 2), ALL)
    placed = (
        P(ALL, None),
        P(ALL, None),
        P(ALL, None, None, None),
        P(ALL, None, None),
        P(ALL, None),
        P(),
        P(ALL, None, None),
        P(ALL, None),
        P(ALL),
        P(ALL, None),
        P(),
    )
    return jax.shard_map(
        per_device,
        mesh=fine,
        in_specs=placed,
        out_specs=(P(ALL, None), P(ALL, None), P(ALL, None), P()),
        check_vma=False,
    )
```

```python
import functools

import jax
import jax.numpy as jnp
from jax import lax
from jax.experimental import pallas as pl
from jax.experimental.pallas import tpu as pltpu
from jax.sharding import Mesh
from jax.sharding import PartitionSpec as P

ALL = ("x", "z", "y", "core")
CHIPS = ("x", "z", "y")
SWAP = ((0, 1), (1, 0))
N_ALL = 128
N_CHIPS = 64
ROOT = 0.7978845608028654
LO = 256
FIELDS = 8
SPAN = 32
SHIFT = 2.0 ** 24
MIB = 1024 * 1024
ROW = 256
GROUP = 2


def in_hbm(*arrays):
    return [pltpu.with_memory_space_constraint(a, pltpu.HBM) for a in arrays]


def in_vmem(*arrays):
    return [pltpu.with_memory_space_constraint(a, pltpu.VMEM) for a in arrays]


def level_of(k):
    return 2.0 ** (24 - 4 * k) if k < FIELDS - 1 else SHIFT


def scale_columns(rows_ref, columns_ref):
    for k in range(FIELDS):
        rows = rows_ref[LO * k : LO * k + LO].astype(jnp.float32) * level_of(k)
        columns_ref[:, LO * k : LO * k + LO] = rows.T.astype(jnp.bfloat16)


def field_counts(word, k):
    if k == FIELDS - 1:
        return lax.shift_right_logical(word, 28).astype(jnp.float32)
    return (word & (15 << (4 * k))).astype(jnp.float32)


def unpack(word, c_ref, base, lanes):
    for k in range(FIELDS):
        c_ref[LO * k + base : LO * k + base + SPAN, lanes] = field_counts(word, k).astype(jnp.bfloat16)


def overlapped(group, samples, fill, dot, c_a, c_b):
    bufs = (c_a, c_b)
    for g in range(group + 1):
        for lane in range(samples // 128):
            lanes = slice(128 * lane, 128 * lane + 128)
            if g > 0 and lane % 2 == 0:
                dot(g - 1, bufs[(g - 1) % 2], slice(128 * lane, 128 * lane + 256))
            if g < group:
                fill(g, bufs[g % 2], lanes)


def count_kernel(start, idx_ref, len_ref, rows_ref, words_ref, part_ref, told_ref, low_ref, old_ref, new_ref, c_a, c_b):
    most, samples = idx_ref.shape[1:]
    line = lax.broadcasted_iota(jnp.int32, (8, 128), 0)
    first = start + GROUP * pl.program_id(0)
    pl.when(pl.program_id(0) == 0)(lambda: scale_columns(rows_ref, told_ref))
    for g in range(GROUP):
        idx = idx_ref[g]
        live = lax.broadcasted_iota(jnp.int32, idx.shape, 0) < len_ref[pl.ds(first + g, 1)]
        high = idx >> 8
        unit = jnp.int32(1) << (4 * (high & 7))
        low = idx & (LO - 1)
        old = jnp.where(live & (high < 8), unit, 0)
        new = jnp.where(live & (high >= 8), unit, 0)
        for j in range(most):
            rows = slice(8 * j, 8 * j + 8)
            low_ref[g, rows] = jnp.broadcast_to(low[j : j + 1], (8, samples))
            old_ref[g, rows] = jnp.broadcast_to(old[j : j + 1], (8, samples))
            new_ref[g, rows] = jnp.broadcast_to(new[j : j + 1], (8, samples))

    def fill(g, c_ref, lanes):
        for base in range(0, LO, SPAN):
            a_old = [jnp.zeros((8, 128), jnp.int32) for _ in range(SPAN // 8)]
            a_new = [jnp.zeros((8, 128), jnp.int32) for _ in range(SPAN // 8)]
            for j in range(most):
                rows = slice(8 * j, 8 * j + 8)
                lo = low_ref[g, rows, lanes] - base
                v_old = old_ref[g, rows, lanes]
                v_new = new_ref[g, rows, lanes]
                for t in range(SPAN // 8):
                    hit = lo == line + 8 * t
                    a_old[t] = a_old[t] + jnp.where(hit, v_old, 0)
                    a_new[t] = a_new[t] + jnp.where(hit, v_new, 0)
            words_ref[g, base : base + SPAN, lanes] = jnp.concatenate(a_new, axis=0)
            unpack(jnp.concatenate(a_old, axis=0), c_ref, base, lanes)

    def dot(g, c_ref, lanes):
        part_ref[g, :, lanes] = jnp.dot(told_ref[...], c_ref[:, lanes], preferred_element_type=jnp.float32)

    overlapped(GROUP, samples, fill, dot, c_a, c_b)


def count_call(idx, length, rows, start, fields):
    _, most, samples = idx.shape
    width = rows.shape[1]
    return pl.pallas_call(
        functools.partial(count_kernel, start),
        grid=(fields // GROUP,),
        in_specs=[
            pl.BlockSpec((GROUP, most, samples), lambda f: (f + start // GROUP, 0, 0)),
            pl.BlockSpec(length.shape, lambda f: (0, 0)),
            pl.BlockSpec(rows.shape, lambda f: (0, 0)),
        ],
        out_specs=[
            pl.BlockSpec((GROUP, LO, samples), lambda f: (f, 0, 0)),
            pl.BlockSpec((GROUP, width, samples), lambda f: (f, 0, 0)),
        ],
        out_shape=[
            pltpu.HBM((fields, LO, samples), jnp.int32),
            pltpu.HBM((fields, width, samples), jnp.float32),
        ],
        scratch_shapes=[
            pltpu.VMEM((width, LO * FIELDS), jnp.bfloat16),
            pltpu.VMEM((GROUP, 8 * most, samples), jnp.int32),
            pltpu.VMEM((GROUP, 8 * most, samples), jnp.int32),
            pltpu.VMEM((GROUP, 8 * most, samples), jnp.int32),
            pltpu.VMEM((LO * FIELDS, samples), jnp.bfloat16),
            pltpu.VMEM((LO * FIELDS, samples), jnp.bfloat16),
        ],
        compiler_params=pltpu.CompilerParams(vmem_limit_bytes=16 * MIB),
        cost_estimate=pl.CostEstimate(flops=2 * fields * samples * 2048 * 128, bytes_accessed=20 << 20, transcendentals=0),
        name="count_bags",
    )(idx, length, rows)


def new_kernel(words_ref, part_ref, rows_ref, across_ref, pooled_ref, tnew_ref, c_a, c_b):
    width, samples = part_ref.shape[1:]

    pl.when(pl.program_id(0) == 0)(lambda: scale_columns(rows_ref, tnew_ref))

    def fill(g, c_ref, lanes):
        for base in range(0, LO, SPAN):
            unpack(words_ref[g, base : base + SPAN, lanes], c_ref, base, lanes)

    def dot(g, c_ref, lanes):
        new = jnp.dot(tnew_ref[...], c_ref[:, lanes], preferred_element_type=jnp.float32)
        both = (part_ref[g, :, lanes] + new) * (1.0 / SHIFT)
        across_ref[width * g : width * g + width, lanes] = both.astype(jnp.bfloat16)
        pooled_ref[lanes, width * g : width * g + width] = both.T.astype(jnp.bfloat16)

    overlapped(GROUP, samples, fill, dot, c_a, c_b)


def new_call(words, part, rows):
    fields, low, samples = words.shape
    width = part.shape[1]
    return pl.pallas_call(
        new_kernel,
        grid=(fields // GROUP,),
        in_specs=[
            pl.BlockSpec((GROUP, low, samples), lambda f: (f, 0, 0)),
            pl.BlockSpec((GROUP, width, samples), lambda f: (f, 0, 0)),
            pl.BlockSpec(rows.shape, lambda f: (0, 0)),
        ],
        out_specs=[
            pl.BlockSpec((width * GROUP, samples), lambda f: (f, 0)),
            pl.BlockSpec((samples, width * GROUP), lambda f: (0, f)),
        ],
        out_shape=[
            pltpu.VMEM((fields * width, samples), jnp.bfloat16),
            pltpu.VMEM((samples, fields * width), jnp.bfloat16),
        ],
        scratch_shapes=[
            pltpu.VMEM((width, LO * FIELDS), jnp.bfloat16),
            pltpu.VMEM((LO * FIELDS, samples), jnp.bfloat16),
            pltpu.VMEM((LO * FIELDS, samples), jnp.bfloat16),
        ],
        compiler_params=pltpu.CompilerParams(vmem_limit_bytes=16 * MIB),
        cost_estimate=pl.CostEstimate(flops=2 * fields * samples * 2048 * 128, bytes_accessed=20 << 20, transcendentals=0),
        name="pool_new",
    )(*in_hbm(words, part), rows)


def hot_kernel(ids_ref, got_ref, hot_ref, table_ref, accum_ref, copies_ref, rows_ref, sems):
    count = ids_ref.shape[1]
    cap = 4
    fetches = []
    for k in range(count):
        row = pl.ds(ids_ref[0, k], 1)
        for which, ref in enumerate((table_ref, accum_ref)):
            fetch = pltpu.make_async_copy(ref.at[row], rows_ref.at[which, pl.ds(k, 1)], sems.at[which, k])
            fetch.start()
            fetches.append(fetch)
    got = got_ref[...]
    total = jnp.zeros((128, 128), jnp.float32)
    for c in range(cap):
        match = (got[:, cap, c : c + 1] == hot_ref[...]).astype(jnp.float32)
        total = total + lax.dot_general(
            match, got[:, c], (((0,), (0,)), ((), ())), precision=lax.Precision.HIGHEST, preferred_element_type=jnp.float32
        )
    total = total[:count]
    for fetch in fetches:
        fetch.wait()
    fresh = rows_ref[0] - 0.5 * total * lax.rsqrt(rows_ref[1] + total * total)
    fresh = fresh.astype(jnp.bfloat16)

    def place(d, carry):
        copies_ref[d] = fresh
        return carry

    lax.fori_loop(0, copies_ref.shape[0], place, 0)


def hot_call(got, ids, table, accum):
    count = ids.shape[1]
    hot = jnp.pad(ids.astype(jnp.float32), ((0, 0), (0, 128 - count)), constant_values=-1.0)
    inside = pl.BlockSpec(memory_space=pltpu.VMEM)
    return pl.pallas_call(
        hot_kernel,
        in_specs=[
            pl.BlockSpec(memory_space=pltpu.SMEM),
            inside,
            inside,
            pl.BlockSpec(memory_space=pltpu.HBM),
            pl.BlockSpec(memory_space=pltpu.HBM),
        ],
        out_specs=inside,
        out_shape=jax.ShapeDtypeStruct((N_ALL, count, 128), jnp.bfloat16),
        scratch_shapes=[pltpu.VMEM((2, count, 128), jnp.float32), pltpu.SemaphoreType.DMA((2, count))],
        compiler_params=pltpu.CompilerParams(vmem_limit_bytes=8 * MIB),
        cost_estimate=pl.CostEstimate(flops=4 * 128**3 * 12, bytes_accessed=1 << 20, transcendentals=count * 128),
        name="hot_rows",
    )(ids, got, hot, *in_hbm(table, accum))


def dense_kernel(
    core_ref, own_a, peer_a, own_b, peer_b, weight_ref, out_ref, act_ref, slope_ref, logit_ref,
    sum_ref, columns_ref, sems,
):
    samples, deep = own_a.shape
    steps = columns_ref.shape[0]
    fetch_columns = []
    for n in range(steps):
        columns = pl.ds(pl.multiple_of(core_ref[0] * (256 * steps) + 256 * n, 256), 256)
        fetch_columns.append(pltpu.make_async_copy(weight_ref.at[:, columns], columns_ref.at[n], sems.at[n]))
    for fetch in fetch_columns:
        fetch.start()

    def product(n, m):
        left, right = ((own_a, own_b), (peer_a, peer_b))[m // 2]
        rows = slice(ROW * (m % 2), ROW * (m % 2) + ROW)
        hidden = jnp.dot(left[rows], columns_ref[n, :deep], preferred_element_type=jnp.float32)
        return hidden + jnp.dot(right[rows], columns_ref[n, deep:], preferred_element_type=jnp.float32)

    def finish(n, m, hidden):
        w = out_ref[:, 256 * n : 256 * n + 256]
        square = hidden * hidden
        t = jnp.tanh(hidden * (ROOT + ROOT * 0.044715 * square))
        near = 0.5 + 0.5 * t
        value = hidden * near
        act = value.astype(jnp.bfloat16)
        slope = near + value * (1.0 - near) * (2.0 * ROOT + 6.0 * ROOT * 0.044715 * square)
        here = slice(ROW * m, ROW * m + ROW)
        act_ref[n, here] = act
        slope_ref[n, here] = slope * w
        term = act.astype(jnp.float32) * w
        term = term[:, :128] + term[:, 128:]
        sum_ref[here] = term if n == 0 else sum_ref[here] + term

    before = None
    for n in range(steps):
        fetch_columns[n].wait()
        for m in range(4):
            hidden = product(n, m)
            if before is not None:
                finish(*before)
            before = (n, m, hidden)
    finish(*before)
    ones = jnp.ones((8, 128), jnp.float32)
    for b in range(logit_ref.shape[0]):
        term = sum_ref[128 * b : 128 * b + 128]
        line = lax.dot_general(
            ones, term, (((1,), (1,)), ((), ())), precision=lax.Precision.HIGHEST, preferred_element_type=jnp.float32
        )
        logit_ref[b : b + 1] = line[:1]


def dense_call(core, own_a, peer_a, own_b, peer_b, weight, out_w):
    samples, deep = own_a.shape
    wide = out_w.shape[0]
    steps = wide // 256
    far = pl.BlockSpec(memory_space=pltpu.HBM)
    inside = pl.BlockSpec(memory_space=pltpu.VMEM)
    return pl.pallas_call(
        dense_kernel,
        in_specs=[pl.BlockSpec(memory_space=pltpu.SMEM)] + [inside] * 4 + [far] + [inside],
        out_specs=[inside] * 3,
        out_shape=[
            pltpu.VMEM((steps, 2 * samples, 256), jnp.bfloat16),
            pltpu.VMEM((steps, 2 * samples, 256), jnp.float32),
            jax.ShapeDtypeStruct((2 * samples // 128, 128), jnp.float32),
        ],
        scratch_shapes=[
            pltpu.VMEM((2 * samples, 128), jnp.float32),
            pltpu.VMEM((steps, 2 * deep, 256), jnp.bfloat16),
            pltpu.SemaphoreType.DMA((steps,)),
        ],
        compiler_params=pltpu.CompilerParams(vmem_limit_bytes=16 * MIB),
        cost_estimate=pl.CostEstimate(flops=4 * samples * deep * 2 * wide, bytes_accessed=14 << 20, transcendentals=2 * samples * wide),
        name="dense_forward",
    )(core.reshape(1), *in_vmem(own_a, peer_a, own_b, peer_b), *in_hbm(weight), out_w.reshape(1, wide))


def grad_kernel(
    own_a, peer_a, own_b, peer_b, act_ref, slope_ref, logit_ref, swapped_ref, marks_ref, out_ref,
    dh_ref, blocks_ref, out_sems,
):
    deep, samples = own_a.shape
    steps = act_ref.shape[0]
    tall = blocks_ref.shape[1]
    own_rows = samples // 128
    logit = logit_ref[...] + jnp.concatenate([swapped_ref[own_rows:], swapped_ref[:own_rows]], axis=0)
    error = (0.125 * (jax.nn.sigmoid(logit) - marks_ref[...])).T
    sent = []
    lines = []
    for c in range(steps):
        total = jnp.zeros((8, 256), jnp.float32)
        for b in range(2 * own_rows):
            rows = slice(128 * b, 128 * b + 128)
            column = error[:, b : b + 1]
            dh_ref[c, rows] = (column * slope_ref[c, rows]).astype(jnp.bfloat16)
            weighted = column * act_ref[c, rows].astype(jnp.float32)
            total = total + jnp.sum(weighted.reshape(16, 8, 256), axis=0)
        total = jnp.sum(total, axis=0, keepdims=True)
        lines += [total[:, :128], total[:, 128:]]
        if c == steps - 1:
            extra = jnp.concatenate(lines, axis=0).astype(jnp.bfloat16)

            def place(d, carry):
                blocks_ref[d, 32 * steps :] = extra
                return carry

            lax.fori_loop(0, blocks_ref.shape[0], place, 0)
        for side in range(2):
            own, peer = ((own_a, peer_a), (own_b, peer_b))[side]
            term = jnp.dot(own[...], dh_ref[c, :samples], preferred_element_type=jnp.float32)
            term = term + jnp.dot(peer[...], dh_ref[c, samples:], preferred_element_type=jnp.float32)
            term = term.astype(jnp.bfloat16)
            blocks = pl.ds(side * (deep // 16), deep // 16)
            for part in range(2):
                at = 32 * c + 16 * part
                blocks_ref[blocks, at : at + 16] = term[:, 128 * part : 128 * part + 128].reshape(-1, 16, 128)
            span = pl.ds(32 * c, (tall - 32 * c) if c == steps - 1 else 32)
            send = pltpu.make_async_copy(blocks_ref.at[blocks, span], out_ref.at[blocks, span], out_sems.at[side, c])
            send.start()
            sent.append(send)
    for send in sent:
        send.wait()


def grad_call(own_a, peer_a, own_b, peer_b, act, slope, logit, swapped, marks):
    deep, samples = own_a.shape
    steps = act.shape[0]
    far = pl.BlockSpec(memory_space=pltpu.HBM)
    inside = pl.BlockSpec(memory_space=pltpu.VMEM)
    shape = (2 * deep // 16, 32 * steps + 8, 128)
    return pl.pallas_call(
        grad_kernel,
        in_specs=[inside] * 9,
        out_specs=far,
        out_shape=pltpu.HBM(shape, jnp.bfloat16),
        scratch_shapes=[
            pltpu.VMEM(act.shape, jnp.bfloat16),
            pltpu.VMEM(shape, jnp.bfloat16),
            pltpu.SemaphoreType.DMA((2, steps)),
        ],
        compiler_params=pltpu.CompilerParams(vmem_limit_bytes=16 * MIB),
        cost_estimate=pl.CostEstimate(flops=8 * samples * deep * 256 * steps, bytes_accessed=14 << 20, transcendentals=0),
        name="grad_terms",
    )(*in_vmem(own_a, peer_a, own_b, peer_b, act, slope), logit, swapped, marks)


def sum_kernel(terms_ref, grad_ref, out_ref, total_ref):
    step = pl.program_id(0)
    chips = terms_ref.shape[0] // 2
    tall = terms_ref.shape[1]
    rows = grad_ref.shape[0]
    half = grad_ref.shape[1] // 2
    for core in range(2):
        for top in range(0, tall, 8):
            part = jnp.zeros((8, 128), jnp.float32)
            for chip in range(chips):
                part = part + terms_ref[2 * chip + core, top : top + 8].astype(jnp.float32)
            span = slice(top, top + 8)
            total_ref[core, span] = jnp.where(step == 0, part, total_ref[core, span] + part)

    @pl.when(step == pl.num_programs(0) - 1)
    def _():
        for core in range(2):
            for c in range(half // 128):
                at = half * core + 128 * c
                grad_ref[:, at : at + 128] = total_ref[core, rows * c : rows * c + rows]
            out_ref[8 * core : 8 * core + 8] = total_ref[core, tall - 8 :]


def sum_call(terms, rows, wide):
    devices, tall, _ = terms.shape
    steps = 4
    return pl.pallas_call(
        sum_kernel,
        grid=(steps,),
        in_specs=[pl.BlockSpec((devices // steps, tall, 128), lambda n: (n, 0, 0))],
        out_specs=[pl.BlockSpec((rows, wide), lambda n: (0, 0)), pl.BlockSpec((16, 128), lambda n: (0, 0))],
        out_shape=[jax.ShapeDtypeStruct((rows, wide), jnp.float32), jax.ShapeDtypeStruct((16, 128), jnp.float32)],
        scratch_shapes=[pltpu.VMEM((2, tall, 128), jnp.float32)],
        compiler_params=pltpu.CompilerParams(vmem_limit_bytes=56 * MIB),
        cost_estimate=pl.CostEstimate(flops=devices * tall * 128, bytes_accessed=5 << 20, transcendentals=0),
        name="sum_terms",
    )(terms)


def per_device(
    table, accum, evict_delta, evict_ids, hot_ids, cache_old, bag_index, bag_length, labels, w_first, w_out
):
    width = table.shape[1]
    cap = evict_ids.shape[2]
    core = lax.axis_index("core")
    half = w_first.shape[1] // 2
    rows = w_first.shape[0]

    numbers = jnp.pad(evict_ids[0].astype(jnp.float32), ((0, 0), (0, width - cap)))[:, None, :]
    blank = jnp.zeros((N_ALL, 8 - cap - 1, width), jnp.float32)
    packet = jnp.concatenate([evict_delta[0], numbers, blank], axis=1)
    got = lax.all_to_all(packet, ALL, split_axis=0, concat_axis=0, tiled=True)

    weight = lax.all_gather(w_first, ALL, axis=0, tiled=True)

    index, length = jnp.transpose(bag_index, (1, 2, 0)), bag_length.T
    fields = index.shape[0]
    first = count_call(index, length, cache_old, 0, fields // 2)
    got, *first = lax.optimization_barrier((got, *first))
    got_delta = got[:, :cap].reshape(-1, width)
    got_ids = got[:, cap, :cap].astype(jnp.int32).reshape(-1)

    copies = hot_call(got, hot_ids, table, accum)
    new_rows = lax.all_to_all(copies, ALL, split_axis=0, concat_axis=0, tiled=True).reshape(-1, width)

    second = count_call(index, length, cache_old, fields // 2, fields // 2)
    across, upright = [], []
    for words, part in (first, second):
        own = new_call(words, part, new_rows)
        for side, store in zip(own, (across, upright)):
            store += [side, lax.ppermute(side, "core", SWAP)]
    marks = labels.astype(jnp.float32).reshape(-1, 128)
    marks = jnp.concatenate([marks, lax.ppermute(marks, "core", SWAP)], axis=0)

    out_w = lax.dynamic_slice_in_dim(w_out, core * half, half)
    act, slope, logit = dense_call(core, *upright, weight, out_w.astype(jnp.float32))
    swapped = lax.ppermute(logit, "core", SWAP)

    blocks = grad_call(*across, act, slope, logit, swapped, marks)
    terms = lax.all_to_all(blocks, ALL, split_axis=0, concat_axis=0, tiled=True)
    grad_w1, out_lines = sum_call(terms, rows, 2 * half)
    grad_w2 = out_lines.reshape(-1)

    summed = jnp.zeros_like(table).at[got_ids].add(got_delta)
    accum_new = accum + summed * summed
    table_new = table - 0.5 * summed * lax.rsqrt(accum_new)
    return (table_new, accum_new, grad_w1, grad_w2)


def solution(mesh):
    fine = Mesh(mesh.devices.reshape(4, 4, 4, 2), ALL)
    placed = (
        P(ALL, None),
        P(ALL, None),
        P(ALL, None, None, None),
        P(ALL, None, None),
        P(ALL, None),
        P(),
        P(ALL, None, None),
        P(ALL, None),
        P(ALL),
        P(ALL, None),
        P(),
    )
    return jax.shard_map(
        per_device,
        mesh=fine,
        in_specs=placed,
        out_specs=(P(ALL, None), P(ALL, None), P(ALL, None), P()),
        check_vma=False,
    )
```

```python
import functools

import jax
import jax.numpy as jnp
from jax import lax
from jax.experimental import pallas as pl
from jax.experimental.pallas import tpu as pltpu
from jax.sharding import Mesh
from jax.sharding import PartitionSpec as P

ALL = ("x", "z", "y", "core")
CHIPS = ("x", "z", "y")
SWAP = ((0, 1), (1, 0))
N_ALL = 128
N_CHIPS = 64
ROOT = 0.7978845608028654
LO = 256
FIELDS = 8
SPAN = 32
SHIFT = 2.0 ** 24
MIB = 1024 * 1024
ROW = 256
GROUP = 2


def in_hbm(*arrays):
    return [pltpu.with_memory_space_constraint(a, pltpu.HBM) for a in arrays]


def in_vmem(*arrays):
    return [pltpu.with_memory_space_constraint(a, pltpu.VMEM) for a in arrays]


def level_of(k):
    return 2.0 ** (24 - 4 * k) if k < FIELDS - 1 else SHIFT


def scale_columns(rows_ref, columns_ref):
    for k in range(FIELDS):
        rows = rows_ref[LO * k : LO * k + LO].astype(jnp.float32) * level_of(k)
        columns_ref[:, LO * k : LO * k + LO] = rows.T.astype(jnp.bfloat16)


def field_counts(word, k):
    if k == FIELDS - 1:
        return lax.shift_right_logical(word, 28).astype(jnp.float32)
    return (word & (15 << (4 * k))).astype(jnp.float32)


def unpack(word, c_ref, base, lanes):
    for k in range(FIELDS):
        c_ref[LO * k + base : LO * k + base + SPAN, lanes] = field_counts(word, k).astype(jnp.bfloat16)


def overlapped(group, samples, fill, dot, c_a, c_b):
    bufs = (c_a, c_b)
    for g in range(group + 1):
        for lane in range(samples // 128):
            lanes = slice(128 * lane, 128 * lane + 128)
            if g > 0 and lane % 2 == 0:
                dot(g - 1, bufs[(g - 1) % 2], slice(128 * lane, 128 * lane + 256))
            if g < group:
                fill(g, bufs[g % 2], lanes)


def count_kernel(start, idx_ref, len_ref, rows_ref, words_ref, part_ref, told_ref, low_ref, old_ref, new_ref, c_a, c_b):
    most, samples = idx_ref.shape[1:]
    line = lax.broadcasted_iota(jnp.int32, (8, 128), 0)
    first = start + GROUP * pl.program_id(0)
    pl.when(pl.program_id(0) == 0)(lambda: scale_columns(rows_ref, told_ref))
    for g in range(GROUP):
        idx = idx_ref[g]
        live = lax.broadcasted_iota(jnp.int32, idx.shape, 0) < len_ref[pl.ds(first + g, 1)]
        high = idx >> 8
        unit = jnp.int32(1) << (4 * (high & 7))
        low = idx & (LO - 1)
        old = jnp.where(live & (high < 8), unit, 0)
        new = jnp.where(live & (high >= 8), unit, 0)
        for j in range(most):
            rows = slice(8 * j, 8 * j + 8)
            low_ref[g, rows] = jnp.broadcast_to(low[j : j + 1], (8, samples))
            old_ref[g, rows] = jnp.broadcast_to(old[j : j + 1], (8, samples))
            new_ref[g, rows] = jnp.broadcast_to(new[j : j + 1], (8, samples))

    def fill(g, c_ref, lanes):
        for base in range(0, LO, SPAN):
            a_old = [jnp.zeros((8, 128), jnp.int32) for _ in range(SPAN // 8)]
            a_new = [jnp.zeros((8, 128), jnp.int32) for _ in range(SPAN // 8)]
            for j in range(most):
                rows = slice(8 * j, 8 * j + 8)
                lo = low_ref[g, rows, lanes] - base
                v_old = old_ref[g, rows, lanes]
                v_new = new_ref[g, rows, lanes]
                for t in range(SPAN // 8):
                    hit = lo == line + 8 * t
                    a_old[t] = a_old[t] + jnp.where(hit, v_old, 0)
                    a_new[t] = a_new[t] + jnp.where(hit, v_new, 0)
            words_ref[g, base : base + SPAN, lanes] = jnp.concatenate(a_new, axis=0)
            unpack(jnp.concatenate(a_old, axis=0), c_ref, base, lanes)

    def dot(g, c_ref, lanes):
        part_ref[g, :, lanes] = jnp.dot(told_ref[...], c_ref[:, lanes], preferred_element_type=jnp.float32)

    overlapped(GROUP, samples, fill, dot, c_a, c_b)


def count_call(idx, length, rows, start, fields):
    _, most, samples = idx.shape
    width = rows.shape[1]
    return pl.pallas_call(
        functools.partial(count_kernel, start),
        grid=(fields // GROUP,),
        in_specs=[
            pl.BlockSpec((GROUP, most, samples), lambda f: (f + start // GROUP, 0, 0)),
            pl.BlockSpec(length.shape, lambda f: (0, 0)),
            pl.BlockSpec(rows.shape, lambda f: (0, 0)),
        ],
        out_specs=[
            pl.BlockSpec((GROUP, LO, samples), lambda f: (f, 0, 0)),
            pl.BlockSpec((GROUP, width, samples), lambda f: (f, 0, 0)),
        ],
        out_shape=[
            pltpu.HBM((fields, LO, samples), jnp.int32),
            pltpu.HBM((fields, width, samples), jnp.float32),
        ],
        scratch_shapes=[
            pltpu.VMEM((width, LO * FIELDS), jnp.bfloat16),
            pltpu.VMEM((GROUP, 8 * most, samples), jnp.int32),
            pltpu.VMEM((GROUP, 8 * most, samples), jnp.int32),
            pltpu.VMEM((GROUP, 8 * most, samples), jnp.int32),
            pltpu.VMEM((LO * FIELDS, samples), jnp.bfloat16),
            pltpu.VMEM((LO * FIELDS, samples), jnp.bfloat16),
        ],
        compiler_params=pltpu.CompilerParams(vmem_limit_bytes=16 * MIB),
        cost_estimate=pl.CostEstimate(flops=2 * fields * samples * 2048 * 128, bytes_accessed=20 << 20, transcendentals=0),
        name="count_bags",
    )(idx, length, rows)


def new_kernel(words_ref, part_ref, rows_ref, across_ref, pooled_ref, tnew_ref, c_a, c_b):
    width, samples = part_ref.shape[1:]

    pl.when(pl.program_id(0) == 0)(lambda: scale_columns(rows_ref, tnew_ref))

    def fill(g, c_ref, lanes):
        for base in range(0, LO, SPAN):
            unpack(words_ref[g, base : base + SPAN, lanes], c_ref, base, lanes)

    def dot(g, c_ref, lanes):
        new = jnp.dot(tnew_ref[...], c_ref[:, lanes], preferred_element_type=jnp.float32)
        both = (part_ref[g, :, lanes] + new) * (1.0 / SHIFT)
        across_ref[width * g : width * g + width, lanes] = both.astype(jnp.bfloat16)
        pooled_ref[lanes, width * g : width * g + width] = both.T.astype(jnp.bfloat16)

    overlapped(GROUP, samples, fill, dot, c_a, c_b)


def new_call(words, part, rows):
    fields, low, samples = words.shape
    width = part.shape[1]
    return pl.pallas_call(
        new_kernel,
        grid=(fields // GROUP,),
        in_specs=[
            pl.BlockSpec((GROUP, low, samples), lambda f: (f, 0, 0)),
            pl.BlockSpec((GROUP, width, samples), lambda f: (f, 0, 0)),
            pl.BlockSpec(rows.shape, lambda f: (0, 0)),
        ],
        out_specs=[
            pl.BlockSpec((width * GROUP, samples), lambda f: (f, 0)),
            pl.BlockSpec((samples, width * GROUP), lambda f: (0, f)),
        ],
        out_shape=[
            pltpu.VMEM((fields * width, samples), jnp.bfloat16),
            pltpu.VMEM((samples, fields * width), jnp.bfloat16),
        ],
        scratch_shapes=[
            pltpu.VMEM((width, LO * FIELDS), jnp.bfloat16),
            pltpu.VMEM((LO * FIELDS, samples), jnp.bfloat16),
            pltpu.VMEM((LO * FIELDS, samples), jnp.bfloat16),
        ],
        compiler_params=pltpu.CompilerParams(vmem_limit_bytes=16 * MIB),
        cost_estimate=pl.CostEstimate(flops=2 * fields * samples * 2048 * 128, bytes_accessed=20 << 20, transcendentals=0),
        name="pool_new",
    )(*in_hbm(words, part), rows)


def hot_kernel(ids_ref, got_ref, hot_ref, table_ref, accum_ref, copies_ref, rows_ref, sems):
    count = ids_ref.shape[1]
    cap = 4
    fetches = []
    for k in range(count):
        row = pl.ds(ids_ref[0, k], 1)
        for which, ref in enumerate((table_ref, accum_ref)):
            fetch = pltpu.make_async_copy(ref.at[row], rows_ref.at[which, pl.ds(k, 1)], sems.at[which, k])
            fetch.start()
            fetches.append(fetch)
    got = got_ref[...]
    total = jnp.zeros((128, 128), jnp.float32)
    for c in range(cap):
        match = (got[:, cap, c : c + 1] == hot_ref[...]).astype(jnp.float32)
        total = total + lax.dot_general(
            match, got[:, c], (((0,), (0,)), ((), ())), precision=lax.Precision.HIGHEST, preferred_element_type=jnp.float32
        )
    total = total[:count]
    for fetch in fetches:
        fetch.wait()
    fresh = rows_ref[0] - 0.5 * total * lax.rsqrt(rows_ref[1] + total * total)
    fresh = fresh.astype(jnp.bfloat16)

    def place(d, carry):
        copies_ref[d] = fresh
        return carry

    lax.fori_loop(0, copies_ref.shape[0], place, 0)


def hot_call(got, ids, table, accum):
    count = ids.shape[1]
    hot = jnp.pad(ids.astype(jnp.float32), ((0, 0), (0, 128 - count)), constant_values=-1.0)
    inside = pl.BlockSpec(memory_space=pltpu.VMEM)
    return pl.pallas_call(
        hot_kernel,
        in_specs=[
            pl.BlockSpec(memory_space=pltpu.SMEM),
            inside,
            inside,
            pl.BlockSpec(memory_space=pltpu.HBM),
            pl.BlockSpec(memory_space=pltpu.HBM),
        ],
        out_specs=inside,
        out_shape=jax.ShapeDtypeStruct((N_ALL, count, 128), jnp.bfloat16),
        scratch_shapes=[pltpu.VMEM((2, count, 128), jnp.float32), pltpu.SemaphoreType.DMA((2, count))],
        compiler_params=pltpu.CompilerParams(vmem_limit_bytes=8 * MIB),
        cost_estimate=pl.CostEstimate(flops=4 * 128**3 * 12, bytes_accessed=1 << 20, transcendentals=count * 128),
        name="hot_rows",
    )(ids, got, hot, *in_hbm(table, accum))


def dense_kernel(
    core_ref, own_a, peer_a, own_b, peer_b, weight_ref, out_ref, act_ref, slope_ref, logit_ref,
    sum_ref, columns_ref, sems,
):
    samples, deep = own_a.shape
    steps = columns_ref.shape[0]
    fetch_columns = []
    for n in range(steps):
        columns = pl.ds(pl.multiple_of(core_ref[0] * (256 * steps) + 256 * n, 256), 256)
        fetch_columns.append(pltpu.make_async_copy(weight_ref.at[:, columns], columns_ref.at[n], sems.at[n]))
    for fetch in fetch_columns:
        fetch.start()

    def product(n, m):
        left, right = ((own_a, own_b), (peer_a, peer_b))[m // 2]
        rows = slice(ROW * (m % 2), ROW * (m % 2) + ROW)
        hidden = jnp.dot(left[rows], columns_ref[n, :deep], preferred_element_type=jnp.float32)
        return hidden + jnp.dot(right[rows], columns_ref[n, deep:], preferred_element_type=jnp.float32)

    def finish(n, m, hidden):
        w = out_ref[:, 256 * n : 256 * n + 256]
        square = hidden * hidden
        t = jnp.tanh(hidden * (ROOT + ROOT * 0.044715 * square))
        near = 0.5 + 0.5 * t
        value = hidden * near
        act = value.astype(jnp.bfloat16)
        slope = near + value * (1.0 - near) * (2.0 * ROOT + 6.0 * ROOT * 0.044715 * square)
        here = slice(ROW * m, ROW * m + ROW)
        act_ref[n, here] = act
        slope_ref[n, here] = slope * w
        term = act.astype(jnp.float32) * w
        term = term[:, :128] + term[:, 128:]
        sum_ref[here] = term if n == 0 else sum_ref[here] + term

    before = None
    for n in range(steps):
        fetch_columns[n].wait()
        for m in range(4):
            hidden = product(n, m)
            if before is not None:
                finish(*before)
            before = (n, m, hidden)
    finish(*before)
    ones = jnp.ones((8, 128), jnp.float32)
    for b in range(logit_ref.shape[0]):
        term = sum_ref[128 * b : 128 * b + 128]
        line = lax.dot_general(
            ones, term, (((1,), (1,)), ((), ())), precision=lax.Precision.HIGHEST, preferred_element_type=jnp.float32
        )
        logit_ref[b : b + 1] = line[:1]


def dense_call(core, own_a, peer_a, own_b, peer_b, weight, out_w):
    samples, deep = own_a.shape
    wide = out_w.shape[0]
    steps = wide // 256
    far = pl.BlockSpec(memory_space=pltpu.HBM)
    inside = pl.BlockSpec(memory_space=pltpu.VMEM)
    return pl.pallas_call(
        dense_kernel,
        in_specs=[pl.BlockSpec(memory_space=pltpu.SMEM)] + [inside] * 4 + [far] + [inside],
        out_specs=[inside] * 3,
        out_shape=[
            pltpu.VMEM((steps, 2 * samples, 256), jnp.bfloat16),
            pltpu.VMEM((steps, 2 * samples, 256), jnp.float32),
            jax.ShapeDtypeStruct((2 * samples // 128, 128), jnp.float32),
        ],
        scratch_shapes=[
            pltpu.VMEM((2 * samples, 128), jnp.float32),
            pltpu.VMEM((steps, 2 * deep, 256), jnp.bfloat16),
            pltpu.SemaphoreType.DMA((steps,)),
        ],
        compiler_params=pltpu.CompilerParams(vmem_limit_bytes=16 * MIB),
        cost_estimate=pl.CostEstimate(flops=4 * samples * deep * 2 * wide, bytes_accessed=14 << 20, transcendentals=2 * samples * wide),
        name="dense_forward",
    )(core.reshape(1), *in_vmem(own_a, peer_a, own_b, peer_b), *in_hbm(weight), out_w.reshape(1, wide))


def grad_kernel(
    own_a, peer_a, own_b, peer_b, act_ref, slope_ref, logit_ref, swapped_ref, marks_ref, out_ref,
    dh_ref, blocks_ref, out_sems,
):
    deep, samples = own_a.shape
    steps = act_ref.shape[0]
    tall = blocks_ref.shape[1]
    own_rows = samples // 128
    logit = logit_ref[...] + jnp.concatenate([swapped_ref[own_rows:], swapped_ref[:own_rows]], axis=0)
    error = (0.125 * (jax.nn.sigmoid(logit) - marks_ref[...])).T
    sent = []
    lines = []
    for c in range(steps):
        total = jnp.zeros((8, 256), jnp.float32)
        for b in range(2 * own_rows):
            rows = slice(128 * b, 128 * b + 128)
            column = error[:, b : b + 1]
            dh_ref[c, rows] = (column * slope_ref[c, rows]).astype(jnp.bfloat16)
            weighted = column * act_ref[c, rows].astype(jnp.float32)
            total = total + jnp.sum(weighted.reshape(16, 8, 256), axis=0)
        total = jnp.sum(total, axis=0, keepdims=True)
        lines += [total[:, :128], total[:, 128:]]
        if c == steps - 1:
            extra = jnp.concatenate(lines, axis=0).astype(jnp.bfloat16)

            def place(d, carry):
                blocks_ref[d, 32 * steps :] = extra
                return carry

            lax.fori_loop(0, blocks_ref.shape[0], place, 0)
        for side in range(2):
            own, peer = ((own_a, peer_a), (own_b, peer_b))[side]
            term = jnp.dot(own[...], dh_ref[c, :samples], preferred_element_type=jnp.float32)
            term = term + jnp.dot(peer[...], dh_ref[c, samples:], preferred_element_type=jnp.float32)
            term = term.astype(jnp.bfloat16)
            blocks = pl.ds(side * (deep // 16), deep // 16)
            for part in range(2):
                at = 32 * c + 16 * part
                blocks_ref[blocks, at : at + 16] = term[:, 128 * part : 128 * part + 128].reshape(-1, 16, 128)
            span = pl.ds(32 * c, (tall - 32 * c) if c == steps - 1 else 32)
            send = pltpu.make_async_copy(blocks_ref.at[blocks, span], out_ref.at[blocks, span], out_sems.at[side, c])
            send.start()
            sent.append(send)
    for send in sent:
        send.wait()


def grad_call(own_a, peer_a, own_b, peer_b, act, slope, logit, swapped, marks):
    deep, samples = own_a.shape
    steps = act.shape[0]
    far = pl.BlockSpec(memory_space=pltpu.HBM)
    inside = pl.BlockSpec(memory_space=pltpu.VMEM)
    shape = (2 * deep // 16, 32 * steps + 8, 128)
    return pl.pallas_call(
        grad_kernel,
        in_specs=[inside] * 9,
        out_specs=far,
        out_shape=pltpu.HBM(shape, jnp.bfloat16),
        scratch_shapes=[
            pltpu.VMEM(act.shape, jnp.bfloat16),
            pltpu.VMEM(shape, jnp.bfloat16),
            pltpu.SemaphoreType.DMA((2, steps)),
        ],
        compiler_params=pltpu.CompilerParams(vmem_limit_bytes=16 * MIB),
        cost_estimate=pl.CostEstimate(flops=8 * samples * deep * 256 * steps, bytes_accessed=14 << 20, transcendentals=0),
        name="grad_terms",
    )(*in_vmem(own_a, peer_a, own_b, peer_b, act, slope), logit, swapped, marks)


def sum_kernel(terms_ref, grad_ref, out_ref, total_ref):
    step = pl.program_id(0)
    chips = terms_ref.shape[0] // 2
    tall = terms_ref.shape[1]
    rows = grad_ref.shape[0]
    half = grad_ref.shape[1] // 2
    for core in range(2):
        for top in range(0, tall, 16):
            size = min(16, tall - top)
            part = jnp.zeros((size, 128), jnp.float32)
            for chip in range(chips):
                part = part + terms_ref[2 * chip + core, top : top + size].astype(jnp.float32)
            span = slice(top, top + size)
            total_ref[core, span] = jnp.where(step == 0, part, total_ref[core, span] + part)

    @pl.when(step == pl.num_programs(0) - 1)
    def _():
        for core in range(2):
            for c in range(half // 128):
                at = half * core + 128 * c
                grad_ref[:, at : at + 128] = total_ref[core, rows * c : rows * c + rows]
            out_ref[8 * core : 8 * core + 8] = total_ref[core, tall - 8 :]


def sum_call(terms, rows, wide):
    devices, tall, _ = terms.shape
    steps = 2
    return pl.pallas_call(
        sum_kernel,
        grid=(steps,),
        in_specs=[pl.BlockSpec((devices // steps, tall, 128), lambda n: (n, 0, 0))],
        out_specs=[pl.BlockSpec((rows, wide), lambda n: (0, 0)), pl.BlockSpec((16, 128), lambda n: (0, 0))],
        out_shape=[jax.ShapeDtypeStruct((rows, wide), jnp.float32), jax.ShapeDtypeStruct((16, 128), jnp.float32)],
        scratch_shapes=[pltpu.VMEM((2, tall, 128), jnp.float32)],
        compiler_params=pltpu.CompilerParams(vmem_limit_bytes=56 * MIB),
        cost_estimate=pl.CostEstimate(flops=devices * tall * 128, bytes_accessed=5 << 20, transcendentals=0),
        name="sum_terms",
    )(terms)


def per_device(
    table, accum, evict_delta, evict_ids, hot_ids, cache_old, bag_index, bag_length, labels, w_first, w_out
):
    width = table.shape[1]
    cap = evict_ids.shape[2]
    core = lax.axis_index("core")
    half = w_first.shape[1] // 2
    rows = w_first.shape[0]

    numbers = jnp.pad(evict_ids[0].astype(jnp.float32), ((0, 0), (0, width - cap)))[:, None, :]
    blank = jnp.zeros((N_ALL, 8 - cap - 1, width), jnp.float32)
    packet = jnp.concatenate([evict_delta[0], numbers, blank], axis=1)
    got = lax.all_to_all(packet, ALL, split_axis=0, concat_axis=0, tiled=True)

    weight = lax.all_gather(w_first, ALL, axis=0, tiled=True)

    index, length = jnp.transpose(bag_index, (1, 2, 0)), bag_length.T
    fields = index.shape[0]
    first = count_call(index, length, cache_old, 0, fields // 2)
    got, *first = lax.optimization_barrier((got, *first))
    got_delta = got[:, :cap].reshape(-1, width)
    got_ids = got[:, cap, :cap].astype(jnp.int32).reshape(-1)

    copies = hot_call(got, hot_ids, table, accum)
    new_rows = lax.all_to_all(copies, ALL, split_axis=0, concat_axis=0, tiled=True).reshape(-1, width)

    second = count_call(index, length, cache_old, fields // 2, fields // 2)
    across, upright = [], []
    for words, part in (first, second):
        own = new_call(words, part, new_rows)
        for side, store in zip(own, (across, upright)):
            store += [side, lax.ppermute(side, "core", SWAP)]
    marks = labels.astype(jnp.float32).reshape(-1, 128)
    marks = jnp.concatenate([marks, lax.ppermute(marks, "core", SWAP)], axis=0)

    out_w = lax.dynamic_slice_in_dim(w_out, core * half, half)
    act, slope, logit = dense_call(core, *upright, weight, out_w.astype(jnp.float32))
    swapped = lax.ppermute(logit, "core", SWAP)

    blocks = grad_call(*across, act, slope, logit, swapped, marks)
    terms = lax.all_to_all(blocks, ALL, split_axis=0, concat_axis=0, tiled=True)
    grad_w1, out_lines = sum_call(terms, rows, 2 * half)
    grad_w2 = out_lines.reshape(-1)

    summed = jnp.zeros_like(table).at[got_ids].add(got_delta)
    accum_new = accum + summed * summed
    table_new = table - 0.5 * summed * lax.rsqrt(accum_new)
    return (table_new, accum_new, grad_w1, grad_w2)


def solution(mesh):
    fine = Mesh(mesh.devices.reshape(4, 4, 4, 2), ALL)
    placed = (
        P(ALL, None),
        P(ALL, None),
        P(ALL, None, None, None),
        P(ALL, None, None),
        P(ALL, None),
        P(),
        P(ALL, None, None),
        P(ALL, None),
        P(ALL),
        P(ALL, None),
        P(),
    )
    return jax.shard_map(
        per_device,
        mesh=fine,
        in_specs=placed,
        out_specs=(P(ALL, None), P(ALL, None), P(ALL, None), P()),
        check_vma=False,
    )
```

```python
import functools

import jax
import jax.numpy as jnp
from jax import lax
from jax.experimental import pallas as pl
from jax.experimental.pallas import tpu as pltpu
from jax.sharding import Mesh
from jax.sharding import PartitionSpec as P

ALL = ("x", "z", "y", "core")
CHIPS = ("x", "z", "y")
SWAP = ((0, 1), (1, 0))
N_ALL = 128
N_CHIPS = 64
ROOT = 0.7978845608028654
LO = 256
FIELDS = 8
SPAN = 32
SHIFT = 2.0 ** 24
MIB = 1024 * 1024
ROW = 256
GROUP = 2


def in_hbm(*arrays):
    return [pltpu.with_memory_space_constraint(a, pltpu.HBM) for a in arrays]


def in_vmem(*arrays):
    return [pltpu.with_memory_space_constraint(a, pltpu.VMEM) for a in arrays]


def level_of(k):
    return 2.0 ** (24 - 4 * k) if k < FIELDS - 1 else SHIFT


def scale_columns(rows_ref, columns_ref):
    for k in range(FIELDS):
        rows = rows_ref[LO * k : LO * k + LO].astype(jnp.float32) * level_of(k)
        columns_ref[:, LO * k : LO * k + LO] = rows.T.astype(jnp.bfloat16)


def field_counts(word, k):
    if k == FIELDS - 1:
        return lax.shift_right_logical(word, 28).astype(jnp.float32)
    return (word & (15 << (4 * k))).astype(jnp.float32)


def unpack(word, c_ref, base, lanes):
    for k in range(FIELDS):
        c_ref[LO * k + base : LO * k + base + SPAN, lanes] = field_counts(word, k).astype(jnp.bfloat16)


def overlapped(group, samples, fill, dot, c_a, c_b):
    bufs = (c_a, c_b)
    for g in range(group + 1):
        for lane in range(samples // 128):
            lanes = slice(128 * lane, 128 * lane + 128)
            if g > 0 and lane % 2 == 0:
                dot(g - 1, bufs[(g - 1) % 2], slice(128 * lane, 128 * lane + 256))
            if g < group:
                fill(g, bufs[g % 2], lanes)


def count_kernel(start, idx_ref, len_ref, rows_ref, words_ref, part_ref, told_ref, low_ref, old_ref, new_ref, c_a, c_b):
    most, samples = idx_ref.shape[1:]
    line = lax.broadcasted_iota(jnp.int32, (8, 128), 0)
    first = start + GROUP * pl.program_id(0)
    pl.when(pl.program_id(0) == 0)(lambda: scale_columns(rows_ref, told_ref))
    for g in range(GROUP):
        idx = idx_ref[g]
        live = lax.broadcasted_iota(jnp.int32, idx.shape, 0) < len_ref[pl.ds(first + g, 1)]
        high = idx >> 8
        unit = jnp.int32(1) << (4 * (high & 7))
        low = idx & (LO - 1)
        old = jnp.where(live & (high < 8), unit, 0)
        new = jnp.where(live & (high >= 8), unit, 0)
        for j in range(most):
            rows = slice(8 * j, 8 * j + 8)
            low_ref[g, rows] = jnp.broadcast_to(low[j : j + 1], (8, samples))
            old_ref[g, rows] = jnp.broadcast_to(old[j : j + 1], (8, samples))
            new_ref[g, rows] = jnp.broadcast_to(new[j : j + 1], (8, samples))

    def fill(g, c_ref, lanes):
        for base in range(0, LO, SPAN):
            a_old = [jnp.zeros((8, 128), jnp.int32) for _ in range(SPAN // 8)]
            a_new = [jnp.zeros((8, 128), jnp.int32) for _ in range(SPAN // 8)]
            for j in range(most):
                rows = slice(8 * j, 8 * j + 8)
                lo = low_ref[g, rows, lanes] - base
                v_old = old_ref[g, rows, lanes]
                v_new = new_ref[g, rows, lanes]
                for t in range(SPAN // 8):
                    hit = lo == line + 8 * t
                    a_old[t] = a_old[t] + jnp.where(hit, v_old, 0)
                    a_new[t] = a_new[t] + jnp.where(hit, v_new, 0)
            words_ref[g, base : base + SPAN, lanes] = jnp.concatenate(a_new, axis=0)
            unpack(jnp.concatenate(a_old, axis=0), c_ref, base, lanes)

    def dot(g, c_ref, lanes):
        part_ref[g, :, lanes] = jnp.dot(told_ref[...], c_ref[:, lanes], preferred_element_type=jnp.float32)

    overlapped(GROUP, samples, fill, dot, c_a, c_b)


def count_call(idx, length, rows, start, fields):
    _, most, samples = idx.shape
    width = rows.shape[1]
    return pl.pallas_call(
        functools.partial(count_kernel, start),
        grid=(fields // GROUP,),
        in_specs=[
            pl.BlockSpec((GROUP, most, samples), lambda f: (f + start // GROUP, 0, 0)),
            pl.BlockSpec(length.shape, lambda f: (0, 0)),
            pl.BlockSpec(rows.shape, lambda f: (0, 0)),
        ],
        out_specs=[
            pl.BlockSpec((GROUP, LO, samples), lambda f: (f, 0, 0)),
            pl.BlockSpec((GROUP, width, samples), lambda f: (f, 0, 0)),
        ],
        out_shape=[
            pltpu.HBM((fields, LO, samples), jnp.int32),
            pltpu.HBM((fields, width, samples), jnp.float32),
        ],
        scratch_shapes=[
            pltpu.VMEM((width, LO * FIELDS), jnp.bfloat16),
            pltpu.VMEM((GROUP, 8 * most, samples), jnp.int32),
            pltpu.VMEM((GROUP, 8 * most, samples), jnp.int32),
            pltpu.VMEM((GROUP, 8 * most, samples), jnp.int32),
            pltpu.VMEM((LO * FIELDS, samples), jnp.bfloat16),
            pltpu.VMEM((LO * FIELDS, samples), jnp.bfloat16),
        ],
        compiler_params=pltpu.CompilerParams(vmem_limit_bytes=16 * MIB),
        cost_estimate=pl.CostEstimate(flops=2 * fields * samples * 2048 * 128, bytes_accessed=20 << 20, transcendentals=0),
        name="count_bags",
    )(idx, length, rows)


def new_kernel(words_ref, part_ref, rows_ref, across_ref, pooled_ref, tnew_ref, c_a, c_b):
    width, samples = part_ref.shape[1:]

    pl.when(pl.program_id(0) == 0)(lambda: scale_columns(rows_ref, tnew_ref))

    def fill(g, c_ref, lanes):
        for base in range(0, LO, SPAN):
            unpack(words_ref[g, base : base + SPAN, lanes], c_ref, base, lanes)

    def dot(g, c_ref, lanes):
        new = jnp.dot(tnew_ref[...], c_ref[:, lanes], preferred_element_type=jnp.float32)
        both = (part_ref[g, :, lanes] + new) * (1.0 / SHIFT)
        across_ref[width * g : width * g + width, lanes] = both.astype(jnp.bfloat16)
        pooled_ref[lanes, width * g : width * g + width] = both.T.astype(jnp.bfloat16)

    overlapped(GROUP, samples, fill, dot, c_a, c_b)


def new_call(words, part, rows):
    fields, low, samples = words.shape
    width = part.shape[1]
    return pl.pallas_call(
        new_kernel,
        grid=(fields // GROUP,),
        in_specs=[
            pl.BlockSpec((GROUP, low, samples), lambda f: (f, 0, 0)),
            pl.BlockSpec((GROUP, width, samples), lambda f: (f, 0, 0)),
            pl.BlockSpec(rows.shape, lambda f: (0, 0)),
        ],
        out_specs=[
            pl.BlockSpec((width * GROUP, samples), lambda f: (f, 0)),
            pl.BlockSpec((samples, width * GROUP), lambda f: (0, f)),
        ],
        out_shape=[
            pltpu.VMEM((fields * width, samples), jnp.bfloat16),
            pltpu.VMEM((samples, fields * width), jnp.bfloat16),
        ],
        scratch_shapes=[
            pltpu.VMEM((width, LO * FIELDS), jnp.bfloat16),
            pltpu.VMEM((LO * FIELDS, samples), jnp.bfloat16),
            pltpu.VMEM((LO * FIELDS, samples), jnp.bfloat16),
        ],
        compiler_params=pltpu.CompilerParams(vmem_limit_bytes=16 * MIB),
        cost_estimate=pl.CostEstimate(flops=2 * fields * samples * 2048 * 128, bytes_accessed=20 << 20, transcendentals=0),
        name="pool_new",
    )(*in_hbm(words, part), rows)


def hot_kernel(ids_ref, got_ref, hot_ref, table_ref, accum_ref, copies_ref, rows_ref, sems):
    count = ids_ref.shape[1]
    cap = 4
    fetches = []
    for k in range(count):
        row = pl.ds(ids_ref[0, k], 1)
        for which, ref in enumerate((table_ref, accum_ref)):
            fetch = pltpu.make_async_copy(ref.at[row], rows_ref.at[which, pl.ds(k, 1)], sems.at[which, k])
            fetch.start()
            fetches.append(fetch)
    got = got_ref[...]
    total = jnp.zeros((128, 128), jnp.float32)
    for c in range(cap):
        match = (got[:, cap, c : c + 1] == hot_ref[...]).astype(jnp.float32)
        total = total + lax.dot_general(
            match, got[:, c], (((0,), (0,)), ((), ())), precision=lax.Precision.HIGHEST, preferred_element_type=jnp.float32
        )
    total = total[:count]
    for fetch in fetches:
        fetch.wait()
    fresh = rows_ref[0] - 0.5 * total * lax.rsqrt(rows_ref[1] + total * total)
    fresh = fresh.astype(jnp.bfloat16)

    def place(d, carry):
        copies_ref[d] = fresh
        return carry

    lax.fori_loop(0, copies_ref.shape[0], place, 0)


def hot_call(got, ids, table, accum):
    count = ids.shape[1]
    hot = jnp.pad(ids.astype(jnp.float32), ((0, 0), (0, 128 - count)), constant_values=-1.0)
    inside = pl.BlockSpec(memory_space=pltpu.VMEM)
    return pl.pallas_call(
        hot_kernel,
        in_specs=[
            pl.BlockSpec(memory_space=pltpu.SMEM),
            inside,
            inside,
            pl.BlockSpec(memory_space=pltpu.HBM),
            pl.BlockSpec(memory_space=pltpu.HBM),
        ],
        out_specs=inside,
        out_shape=jax.ShapeDtypeStruct((N_ALL, count, 128), jnp.bfloat16),
        scratch_shapes=[pltpu.VMEM((2, count, 128), jnp.float32), pltpu.SemaphoreType.DMA((2, count))],
        compiler_params=pltpu.CompilerParams(vmem_limit_bytes=8 * MIB),
        cost_estimate=pl.CostEstimate(flops=4 * 128**3 * 12, bytes_accessed=1 << 20, transcendentals=count * 128),
        name="hot_rows",
    )(ids, got, hot, *in_hbm(table, accum))


def stage_kernel(own_a, peer_a, own_b, peer_b, sides_ref, sems):
    fetches = [
        pltpu.make_async_copy(side, sides_ref.at[i], sems.at[i]) for i, side in enumerate((own_a, peer_a, own_b, peer_b))
    ]
    for fetch in fetches:
        fetch.start()
    for fetch in fetches:
        fetch.wait()


def stage_call(*sides):
    samples, deep = sides[0].shape
    return pl.pallas_call(
        stage_kernel,
        in_specs=[pl.BlockSpec(memory_space=pltpu.HBM)] * 4,
        out_specs=pl.BlockSpec(memory_space=pltpu.VMEM),
        out_shape=pltpu.VMEM((4, samples, deep), jnp.bfloat16),
        scratch_shapes=[pltpu.SemaphoreType.DMA((4,))],
        compiler_params=pltpu.CompilerParams(vmem_limit_bytes=8 * MIB),
        cost_estimate=pl.CostEstimate(flops=0, bytes_accessed=8 << 20, transcendentals=0),
        name="stage_rows",
    )(*in_hbm(*sides))


def dense_kernel(
    core_ref, sides_ref, weight_ref, out_ref, act_ref, slope_ref, logit_ref,
    sum_ref, columns_ref, sems,
):
    _, samples, deep = sides_ref.shape
    steps = columns_ref.shape[0]
    fetch_columns = []
    for n in range(steps):
        columns = pl.ds(pl.multiple_of(core_ref[0] * (256 * steps) + 256 * n, 256), 256)
        fetch_columns.append(pltpu.make_async_copy(weight_ref.at[:, columns], columns_ref.at[n], sems.at[n]))
    for fetch in fetch_columns:
        fetch.start()

    def product(n, m):
        left, right = sides_ref.at[m // 2], sides_ref.at[2 + m // 2]
        rows = slice(ROW * (m % 2), ROW * (m % 2) + ROW)
        hidden = jnp.dot(left[rows], columns_ref[n, :deep], preferred_element_type=jnp.float32)
        return hidden + jnp.dot(right[rows], columns_ref[n, deep:], preferred_element_type=jnp.float32)

    def finish(n, m, hidden):
        w = out_ref[:, 256 * n : 256 * n + 256]
        square = hidden * hidden
        t = jnp.tanh(hidden * (ROOT + ROOT * 0.044715 * square))
        near = 0.5 + 0.5 * t
        value = hidden * near
        act = value.astype(jnp.bfloat16)
        slope = near + value * (1.0 - near) * (2.0 * ROOT + 6.0 * ROOT * 0.044715 * square)
        here = slice(ROW * m, ROW * m + ROW)
        act_ref[n, here] = act
        slope_ref[n, here] = slope * w
        term = act.astype(jnp.float32) * w
        term = term[:, :128] + term[:, 128:]
        sum_ref[here] = term if n == 0 else sum_ref[here] + term

    before = None
    for n in range(steps):
        fetch_columns[n].wait()
        for m in range(4):
            hidden = product(n, m)
            if before is not None:
                finish(*before)
            before = (n, m, hidden)
    finish(*before)
    ones = jnp.ones((8, 128), jnp.float32)
    for b in range(logit_ref.shape[0]):
        term = sum_ref[128 * b : 128 * b + 128]
        line = lax.dot_general(
            ones, term, (((1,), (1,)), ((), ())), precision=lax.Precision.HIGHEST, preferred_element_type=jnp.float32
        )
        logit_ref[b : b + 1] = line[:1]


def dense_call(core, own_a, peer_a, own_b, peer_b, weight, out_w):
    samples, deep = own_a.shape
    wide = out_w.shape[0]
    steps = wide // 256
    far = pl.BlockSpec(memory_space=pltpu.HBM)
    inside = pl.BlockSpec(memory_space=pltpu.VMEM)
    return pl.pallas_call(
        dense_kernel,
        in_specs=[pl.BlockSpec(memory_space=pltpu.SMEM)] + [inside] + [far] + [inside],
        out_specs=[inside] * 3,
        out_shape=[
            pltpu.VMEM((steps, 2 * samples, 256), jnp.bfloat16),
            pltpu.VMEM((steps, 2 * samples, 256), jnp.float32),
            jax.ShapeDtypeStruct((2 * samples // 128, 128), jnp.float32),
        ],
        scratch_shapes=[
            pltpu.VMEM((2 * samples, 128), jnp.float32),
            pltpu.VMEM((steps, 2 * deep, 256), jnp.bfloat16),
            pltpu.SemaphoreType.DMA((steps,)),
        ],
        compiler_params=pltpu.CompilerParams(vmem_limit_bytes=16 * MIB),
        cost_estimate=pl.CostEstimate(flops=4 * samples * deep * 2 * wide, bytes_accessed=14 << 20, transcendentals=2 * samples * wide),
        name="dense_forward",
    )(core.reshape(1), *in_vmem(stage_call(own_a, peer_a, own_b, peer_b)), *in_hbm(weight), out_w.reshape(1, wide))


def grad_kernel(
    own_a, peer_a, own_b, peer_b, act_ref, slope_ref, logit_ref, swapped_ref, marks_ref, out_ref,
    dh_ref, blocks_ref, out_sems,
):
    deep, samples = own_a.shape
    steps = act_ref.shape[0]
    tall = blocks_ref.shape[1]
    own_rows = samples // 128
    logit = logit_ref[...] + jnp.concatenate([swapped_ref[own_rows:], swapped_ref[:own_rows]], axis=0)
    error = (0.125 * (jax.nn.sigmoid(logit) - marks_ref[...])).T
    sent = []
    lines = []
    for c in range(steps):
        total = jnp.zeros((8, 256), jnp.float32)
        for b in range(2 * own_rows):
            rows = slice(128 * b, 128 * b + 128)
            column = error[:, b : b + 1]
            dh_ref[c, rows] = (column * slope_ref[c, rows]).astype(jnp.bfloat16)
            weighted = column * act_ref[c, rows].astype(jnp.float32)
            total = total + jnp.sum(weighted.reshape(16, 8, 256), axis=0)
        total = jnp.sum(total, axis=0, keepdims=True)
        lines += [total[:, :128], total[:, 128:]]
        if c == steps - 1:
            extra = jnp.concatenate(lines, axis=0).astype(jnp.bfloat16)

            def place(d, carry):
                blocks_ref[d, 32 * steps :] = extra
                return carry

            lax.fori_loop(0, blocks_ref.shape[0], place, 0)
        for side in range(2):
            own, peer = ((own_a, peer_a), (own_b, peer_b))[side]
            term = jnp.dot(own[...], dh_ref[c, :samples], preferred_element_type=jnp.float32)
            term = term + jnp.dot(peer[...], dh_ref[c, samples:], preferred_element_type=jnp.float32)
            term = term.astype(jnp.bfloat16)
            blocks = pl.ds(side * (deep // 16), deep // 16)
            for part in range(2):
                at = 32 * c + 16 * part
                blocks_ref[blocks, at : at + 16] = term[:, 128 * part : 128 * part + 128].reshape(-1, 16, 128)
            span = pl.ds(32 * c, (tall - 32 * c) if c == steps - 1 else 32)
            send = pltpu.make_async_copy(blocks_ref.at[blocks, span], out_ref.at[blocks, span], out_sems.at[side, c])
            send.start()
            sent.append(send)
    for send in sent:
        send.wait()


def grad_call(own_a, peer_a, own_b, peer_b, act, slope, logit, swapped, marks):
    deep, samples = own_a.shape
    steps = act.shape[0]
    far = pl.BlockSpec(memory_space=pltpu.HBM)
    inside = pl.BlockSpec(memory_space=pltpu.VMEM)
    shape = (2 * deep // 16, 32 * steps + 8, 128)
    return pl.pallas_call(
        grad_kernel,
        in_specs=[inside] * 9,
        out_specs=far,
        out_shape=pltpu.HBM(shape, jnp.bfloat16),
        scratch_shapes=[
            pltpu.VMEM(act.shape, jnp.bfloat16),
            pltpu.VMEM(shape, jnp.bfloat16),
            pltpu.SemaphoreType.DMA((2, steps)),
        ],
        compiler_params=pltpu.CompilerParams(vmem_limit_bytes=16 * MIB),
        cost_estimate=pl.CostEstimate(flops=8 * samples * deep * 256 * steps, bytes_accessed=14 << 20, transcendentals=0),
        name="grad_terms",
    )(*in_vmem(own_a, peer_a, own_b, peer_b, act, slope), logit, swapped, marks)


def sum_kernel(terms_ref, grad_ref, out_ref, total_ref):
    step = pl.program_id(0)
    chips = terms_ref.shape[0] // 2
    tall = terms_ref.shape[1]
    rows = grad_ref.shape[0]
    half = grad_ref.shape[1] // 2
    for core in range(2):
        for top in range(0, tall, 16):
            size = min(16, tall - top)
            part = jnp.zeros((size, 128), jnp.float32)
            for chip in range(chips):
                part = part + terms_ref[2 * chip + core, top : top + size].astype(jnp.float32)
            span = slice(top, top + size)
            total_ref[core, span] = jnp.where(step == 0, part, total_ref[core, span] + part)

    @pl.when(step == pl.num_programs(0) - 1)
    def _():
        for core in range(2):
            for c in range(half // 128):
                at = half * core + 128 * c
                grad_ref[:, at : at + 128] = total_ref[core, rows * c : rows * c + rows]
            out_ref[8 * core : 8 * core + 8] = total_ref[core, tall - 8 :]


def sum_call(terms, rows, wide):
    devices, tall, _ = terms.shape
    steps = 2
    return pl.pallas_call(
        sum_kernel,
        grid=(steps,),
        in_specs=[pl.BlockSpec((devices // steps, tall, 128), lambda n: (n, 0, 0))],
        out_specs=[pl.BlockSpec((rows, wide), lambda n: (0, 0)), pl.BlockSpec((16, 128), lambda n: (0, 0))],
        out_shape=[jax.ShapeDtypeStruct((rows, wide), jnp.float32), jax.ShapeDtypeStruct((16, 128), jnp.float32)],
        scratch_shapes=[pltpu.VMEM((2, tall, 128), jnp.float32)],
        compiler_params=pltpu.CompilerParams(vmem_limit_bytes=56 * MIB),
        cost_estimate=pl.CostEstimate(flops=devices * tall * 128, bytes_accessed=5 << 20, transcendentals=0),
        name="sum_terms",
    )(terms)


def per_device(
    table, accum, evict_delta, evict_ids, hot_ids, cache_old, bag_index, bag_length, labels, w_first, w_out
):
    width = table.shape[1]
    cap = evict_ids.shape[2]
    core = lax.axis_index("core")
    half = w_first.shape[1] // 2
    rows = w_first.shape[0]

    numbers = jnp.pad(evict_ids[0].astype(jnp.float32), ((0, 0), (0, width - cap)))[:, None, :]
    blank = jnp.zeros((N_ALL, 8 - cap - 1, width), jnp.float32)
    packet = jnp.concatenate([evict_delta[0], numbers, blank], axis=1)
    got = lax.all_to_all(packet, ALL, split_axis=0, concat_axis=0, tiled=True)

    weight = lax.all_gather(w_first, ALL, axis=0, tiled=True)

    index, length = jnp.transpose(bag_index, (1, 2, 0)), bag_length.T
    fields = index.shape[0]
    first = count_call(index, length, cache_old, 0, fields // 2)
    got, *first = lax.optimization_barrier((got, *first))
    got_delta = got[:, :cap].reshape(-1, width)
    got_ids = got[:, cap, :cap].astype(jnp.int32).reshape(-1)

    copies = hot_call(got, hot_ids, table, accum)
    new_rows = lax.all_to_all(copies, ALL, split_axis=0, concat_axis=0, tiled=True).reshape(-1, width)

    second = count_call(index, length, cache_old, fields // 2, fields // 2)
    across, upright = [], []
    for words, part in (first, second):
        own = new_call(words, part, new_rows)
        for side, store in zip(own, (across, upright)):
            store += [side, lax.ppermute(side, "core", SWAP)]
    marks = labels.astype(jnp.float32).reshape(-1, 128)
    marks = jnp.concatenate([marks, lax.ppermute(marks, "core", SWAP)], axis=0)

    out_w = lax.dynamic_slice_in_dim(w_out, core * half, half)
    act, slope, logit = dense_call(core, *upright, weight, out_w.astype(jnp.float32))
    swapped = lax.ppermute(logit, "core", SWAP)

    blocks = grad_call(*across, act, slope, logit, swapped, marks)
    terms = lax.all_to_all(blocks, ALL, split_axis=0, concat_axis=0, tiled=True)
    grad_w1, out_lines = sum_call(terms, rows, 2 * half)
    grad_w2 = out_lines.reshape(-1)

    summed = jnp.zeros_like(table).at[got_ids].add(got_delta)
    accum_new = accum + summed * summed
    table_new = table - 0.5 * summed * lax.rsqrt(accum_new)
    return (table_new, accum_new, grad_w1, grad_w2)


def solution(mesh):
    fine = Mesh(mesh.devices.reshape(4, 4, 4, 2), ALL)
    placed = (
        P(ALL, None),
        P(ALL, None),
        P(ALL, None, None, None),
        P(ALL, None, None),
        P(ALL, None),
        P(),
        P(ALL, None, None),
        P(ALL, None),
        P(ALL),
        P(ALL, None),
        P(),
    )
    return jax.shard_map(
        per_device,
        mesh=fine,
        in_specs=placed,
        out_specs=(P(ALL, None), P(ALL, None), P(ALL, None), P()),
        check_vma=False,
    )
```
